512 devices in a mesh: dp: 16 (over z_hi, x, core), shard: 32 (over y, z_lo).
Axes of the slice: x: 4, y: 8, z: 8 (z_hi: 2, z_lo: 4; z = z_hi * 4 + z_lo), core: 2. Of those that a mesh axis runs over, the one named last changes fastest.
Arguments:
- grad_groups: bfloat16 [16, 106496, 256], P('dp', 'shard'), may hold values from -9 to 9
- master: float32 [106496, 256], P(('shard', 'dp')), may hold values from -0.75 to 0.75
- moment1: float32 [106496, 256], P(('shard', 'dp')), may hold values from -0.75 to 0.75
- moment2: float32 [106496, 256], P(('shard', 'dp')), may hold values from 0.001 to 0.1
- proj: bfloat16 [256, 4096], P('dp'), may hold values from -1 to 1
- ln_gain: float32 [4096], replicated, may hold values from 0.25 to 1.75
- w_qkv: bfloat16 [4096, 6144], P('dp', 'shard'), may hold values from -0.09375 to 0.09375
- token_owner: int32 [65536, 1], P(('dp', 'shard')), may hold values from 0 to 31; in each aligned block of 128 rows (0 to 127, 128 to 255, ...) at most 8 rows name the same one
- token_row: int32 [65536], P(('dp', 'shard')), may hold values from 0 to 207
Outputs:
- new_master: float32 [106496, 256], P(('shard', 'dp'))
- new_moment1: float32 [106496, 256], P(('shard', 'dp'))
- new_moment2: float32 [106496, 256], P(('shard', 'dp'))
- qkv: bfloat16 [65536, 6144], P('dp', 'shard')
The draws below stay inside these ranges and needn't reach their ends.
Inputs may be any that keep to these rules, and one draw needn't show every extreme that they name: `token_owner`: of the 128 tokens of one device at most 8 name any one shard block, and some block of every device is named by exactly 8; so at most 1 token of one device fall on one owner of one block, and some owner receives exactly 1 from every device.
All inputs are finite; a program needn't handle non-finite values.
Results may differ from the reference program's by a relative error of at most 0.018.
Values may be sent and summed in bfloat16 or wider, within the bound.
A program may use at most 64 MiB of HBM per device.

```python
import math
import jax
import jax.numpy as jnp
import numpy as np
from jax import lax

E = 256
D = 4096
RB = 208
TOK_DEV = 128
CAP = 8
BLOCK = 3328
VB = 106496
QKV = 6144
GROUP_TOK = 4096
TOKENS = 65536
N_DP = 16
N_SHARD = 32


def draw_grad_groups(key, part):
    key_base = jax.random.fold_in(key, 11)
    key_cols = jax.random.fold_in(key, 12)
    key_block = jax.random.fold_in(key, 14)
    base = jnp.clip(jax.random.normal(key_base, (N_DP, VB, E), jnp.float32), -6.0, 6.0)
    row_scale = jnp.exp(jnp.log(10.0) * jnp.arange(VB, dtype=jnp.float32) / VB)
    block_level = jax.random.uniform(key_block, (VB // RB,), jnp.float32, -1.15, 1.15)
    row_scale = row_scale * jnp.repeat(jnp.exp(block_level), RB)
    col_scale = jnp.exp(jnp.log(10.0) * jax.random.uniform(key_cols, (E,), jnp.float32))
    values = 0.01 * base * row_scale[None, :, None] * col_scale[None, None, :]
    return jnp.clip(values, -9.0, 9.0).astype(jnp.bfloat16)


def draw_proj(key, part):
    key = jax.random.fold_in(key, 21)
    key_common = jax.random.fold_in(key, 1)
    key_own = jax.random.fold_in(key, 2)
    common = jnp.clip(jax.random.normal(key_common, (1, D), jnp.float32), -4.0, 4.0)
    own = jnp.clip(jax.random.normal(key_own, (E, D), jnp.float32), -4.0, 4.0)
    values = (0.5 * common + 0.866 * own) / math.sqrt(E)
    return jnp.clip(values, -1.0, 1.0).astype(jnp.bfloat16)


def with_ends(entries, own_key, smallest, high):
    longest = entries.shape.index(max(entries.shape))
    spots = []
    for shift in (0, 1):
        where = [jax.random.randint(jax.random.fold_in(own_key, axis), (), 0, length) for axis, length in enumerate(entries.shape)]
        where[longest] = (where[longest] + shift) % entries.shape[longest]
        spots.append(tuple(where))
    return entries.at[spots[0]].set(smallest).at[spots[1]].set(high)


def block_scale(rng, dims, shards, smallest, high):
    factor_of = 1.0
    for dim, blocks in shards:
        draws = jax.random.uniform(jax.random.fold_in(jax.random.fold_in(rng, 6), dim), (blocks,), jnp.float32, smallest / len(shards), high / len(shards))
        factor_of = factor_of * jnp.repeat(jnp.exp(draws), dims[dim] // blocks).reshape((-1,) + (1,) * (len(dims) - 1 - dim))
    return factor_of


def deal_out(key, own, number, rows, number_of, top, bound, skew):
    sequence = jax.random.permutation(key, number_of)
    crowded, usual = load_shares(number_of, rows * top, bound, skew, True), load_shares(number_of, rows * top, bound, skew, False)
    places = jnp.arange(number_of)

    def named(lengths, turn):
        used = int((lengths > 0).sum())
        fixed = max(1, used // 4)
        passed = fixed + (places - fixed + turn * (used - fixed)) % max(1, number_of - fixed)
        return jnp.zeros((number_of,), jnp.int32).at[sequence[jnp.where(places < fixed, places, passed)]].set(jnp.asarray(lengths, jnp.int32))

    lengths = jnp.where(number % 4 == 0, named(crowded, number // 4), named(usual, number - number // 4 - 1))
    mixed = jax.random.permutation(jax.random.fold_in(own, 3), number_of)
    source_of, taker = mixed[0:number_of // 2 * 2:2], mixed[1:number_of // 2 * 2:2]
    slack = jnp.minimum(lengths[source_of] - 1, bound - lengths[taker]) // 2
    slack = jnp.where((source_of == sequence[0]) | (taker == sequence[0]) | (lengths[taker] == 0), 0, jnp.maximum(slack, 0))
    passed = jax.random.randint(jax.random.fold_in(own, 4), (number_of // 2,), 0, 1 << 20) % (slack + 1)
    lengths = lengths.at[source_of].add(-passed).at[taker].add(passed)
    labels = jnp.searchsorted(jnp.cumsum(lengths), jnp.arange(rows * top), side="right").astype(jnp.int32)
    grid = labels.reshape(top, rows).T
    grid = grid[jax.random.permutation(jax.random.fold_in(own, 1), rows)]
    turn = jax.random.randint(jax.random.fold_in(own, 2), (rows, 1), 0, top)
    return jnp.take_along_axis(grid, (jnp.arange(top)[None, :] + turn) % top, axis=1)


def load_shares(count, total, bound, skew, full):
    portions = [(1 << 20) // math.isqrt(rank ** skew) + 1 for rank in range(1, count + 1)]
    largest = bound if full else min(bound, max(-(-total // count), total * portions[0] // sum(portions)))
    least = 1 if total - largest >= count - 1 else 0
    holding, spare = [largest] + [least] * (count - 1), total - largest - least * (count - 1)
    while spare > 0:
        free = [i for i in range(1, count) if holding[i] < largest] or [i for i in range(1, count) if holding[i] < bound]
        pool, remaining = sum([portions[i] for i in free]), spare
        for i in free:
            extra = min(bound - holding[i], max(1, remaining * portions[i] // pool), spare)
            holding[i] = holding[i] + extra
            spare = spare - extra
    return np.array(holding)


def centred(own_key, shape, deviation, reach, shards=(), held_as=jnp.bfloat16):
    factor_of = block_scale(own_key, shape, shards, -0.22, 0.18) if shards else 1.0
    entries = jax.random.normal(own_key, shape, jnp.float32) * deviation * factor_of
    return jnp.minimum(jnp.maximum(entries, -reach), reach).astype(held_as)


def setup_inputs(seed: int = 0) -> dict:
    splits = jax.random.split(jax.random.key(seed), 10)
    grad_groups = draw_grad_groups(jax.random.fold_in(splits[9], 71), 0)
    master = centred(splits[1], (VB, E), 0.05, 0.75, ((0, 512),), jnp.float32)
    moment1 = centred(splits[2], (VB, E), 0.05, 0.75, ((0, 512),), jnp.float32)
    moment2 = jnp.clip(jnp.exp(math.log(0.1) - 4.6051702 * jax.random.uniform(splits[3], (VB, E), jnp.float32) ** block_scale(splits[3], (VB, E), ((0, 512),), -0.2, 0.2)), 0.001, 0.1)
    proj = draw_proj(jax.random.fold_in(splits[9], 71), 0)
    ln_gain = jnp.clip(1.0 + 0.15 * jax.random.normal(splits[5], (D,), jnp.float32), 0.25, 1.75)
    w_qkv = centred(splits[6], (D, QKV), D ** -0.5, 0.09375, ((0, 16), (1, 32)))
    token_owner_keys = jax.random.split(jax.random.fold_in(splits[7], 1), TOKENS // TOK_DEV)
    token_owner_turns = jax.random.permutation(jax.random.fold_in(splits[7], 3), TOKENS // TOK_DEV)
    token_owner = jax.vmap(lambda own, number: deal_out(jax.random.fold_in(splits[7], 2), own, number, TOK_DEV, N_SHARD, 1, CAP, 2))(token_owner_keys, token_owner_turns).reshape((TOKENS, 1))
    token_row = with_ends(jax.random.randint(splits[8], (TOKENS,), 0, RB), jax.random.fold_in(splits[8], 1), 0, RB - 1).astype(jnp.int32)
    return dict(grad_groups=grad_groups, master=master, moment1=moment1, moment2=moment2, proj=proj, ln_gain=ln_gain, w_qkv=w_qkv, token_owner=token_owner, token_row=token_row)


def adam_step(summed, master, moment1, moment2, clip_factor):
    grad = clip_factor * summed
    new_moment1 = 0.9 * moment1 + 0.1 * grad
    new_moment2 = 0.95 * moment2 + 0.05 * grad * grad
    fixed_one = new_moment1 / (1.0 - 0.9 ** 10)
    fixed_two = new_moment2 / (1.0 - 0.95 ** 10)
    new_master = master - 0.01 * (fixed_one / (jnp.sqrt(fixed_two) + 1e-08) + 0.1 * master)
    return (new_master, new_moment1, new_moment2)

def reference(grad_groups, master, moment1, moment2, proj, ln_gain, w_qkv, token_owner, token_row):
    summed = jnp.zeros(master.shape, jnp.float32)
    for group in range(N_DP):
        summed = summed + grad_groups[group].astype(jnp.float32)
    total = jnp.sum(summed * summed)
    clip_factor = jnp.minimum(1.0, 0.2 * math.sqrt(VB * E) / (jnp.sqrt(total) + 1e-06))
    new_master, new_moment1, new_moment2 = adam_step(summed, master, moment1, moment2, clip_factor)
    table = new_master.astype(jnp.bfloat16)
    owners = token_owner[:, 0].reshape(N_DP * N_SHARD, TOK_DEV).astype(jnp.int32)
    member = (owners[:, :, None] == jnp.arange(N_SHARD, dtype=jnp.int32)[None, None, :]).astype(jnp.int32)
    places = jnp.cumsum(member, axis=1) - 1
    slot = lax.optimization_barrier(jnp.sum(places * member, axis=2)).astype(jnp.int32)
    sender = (jnp.arange(N_DP * N_SHARD, dtype=jnp.int32) % N_SHARD)[:, None]
    owner_dp = ((slot + sender) % N_DP).astype(jnp.int32)
    within = token_row.reshape(N_DP * N_SHARD, TOK_DEV).astype(jnp.int32)
    index = (owners * BLOCK + owner_dp * RB + within).reshape(TOKENS).astype(jnp.int32)
    rows = table[index]
    proj_float = proj.astype(jnp.float32)
    gram = jnp.dot(proj_float, proj_float.T, precision=lax.Precision.HIGHEST)
    folded = jnp.dot(proj_float * ln_gain[None, :], w_qkv.astype(jnp.float32), precision=lax.Precision.HIGHEST)
    blocks = rows.reshape(N_DP, GROUP_TOK, E)

    def project(block):
        rows_float = block.astype(jnp.float32)
        mean_sq = lax.optimization_barrier(jnp.sum(jnp.dot(rows_float, gram, precision=lax.Precision.HIGHEST) * rows_float, axis=1)) / D
        values = jnp.dot(rows_float, folded, precision=lax.Precision.HIGHEST)
        return (values * lax.rsqrt(mean_sq + 1e-05)[:, None]).astype(jnp.bfloat16)
    qkv = lax.map(project, blocks).reshape(TOKENS, QKV)
    return (new_master, new_moment1, new_moment2, qkv)
```

```python
import math

import jax
import jax.numpy as jnp
from jax import lax
from jax.experimental import pallas as pl
from jax.experimental.pallas import tpu as pltpu
from jax.sharding import PartitionSpec as P

MESH = pl.DeviceIdType.MESH
F32 = jnp.float32
BF16 = jnp.bfloat16
ROWS = 208
PIECES = ((0, 112), (112, 96))
TOTAL_ENTRIES = 106496 * 256


def dot(a, b):
    return lax.dot_general(a, b, (((1,), (0,)), ((), ())), preferred_element_type=F32)


def dot_t(a, b):
    return lax.dot_general(a, b, (((1,), (1,)), ((), ())), preferred_element_type=F32)


def iota(shape, axis):
    return lax.broadcasted_iota(jnp.int32, shape, axis)


def kernel(
    g_ref, master_ref, m1_ref, m2_ref, proj_ref, gain_ref, w_ref, owner_ref, row_ref,
    o_master, o_m1, o_m2, o_q,
    own, buf_a, buf_b1, buf_b2, send_c, buf_c, state, summed_ref,
    tok_mine, tok_all, idx_send, idx_all, onehot, proj_all, part_send, part_all, w_mine, w_all,
    sq1_mine, sq1_all, sq2_mine, sq2_all, rows_send, rows_all, back_send, back_all, gathered,
    local_sem, a_send, a_recv, b1_send, b1_recv, b2_send, b2_recv, c_send, c_recv,
    dp_send, dp_recv, sh_send, sh_recv, z_send, z_recv, y_send, y_recv,
):
    d = lax.axis_index("dp")
    s = lax.axis_index("shard")
    core, x, zh = lax.rem(d, 2), lax.rem(d // 2, 4), d // 8
    y, z = s // 4, lax.rem(s, 4)

    def dp_peer(i):
        kz, kx, kc = i // 8, lax.rem(i // 2, 4), lax.rem(i, 2)
        return lax.rem(zh + kz, 2) * 8 + lax.rem(x + kx, 4) * 2 + lax.rem(core + kc, 2)

    def sh_peer(i):
        return lax.rem(y + i // 4, 8) * 4 + lax.rem(z + lax.rem(i, 4), 4)

    def x_dev(k):
        return (zh * 8 + lax.rem(x + k, 4) * 2 + core, s)

    def y_dev(k):
        return (d, lax.rem(y + k, 8) * 4 + z)

    load_own = pltpu.make_async_copy(g_ref.at[:, :, core], own, local_sem.at[0])
    load_own.start()
    loads = []
    for n, ref in enumerate((master_ref, m1_ref, m2_ref)):
        load = pltpu.make_async_copy(ref, state.at[n], local_sem.at[1 + n])
        load.start()
        loads.append(load)

    barrier = pltpu.get_barrier_semaphore()

    def greet_dp(i, carry):
        pl.semaphore_signal(barrier, inc=1, device_id=(dp_peer(15 - i), s), device_id_type=MESH)
        return carry

    def greet_sh(i, carry):
        pl.semaphore_signal(barrier, inc=1, device_id=(d, sh_peer(31 - i)), device_id_type=MESH)
        return carry

    lax.fori_loop(0, 31, greet_sh, 0)
    lax.fori_loop(0, 15, greet_dp, 0)
    pl.semaphore_wait(barrier, 46)

    finish = []

    def remote(src, dst, send_sem, recv_sem, device):
        copy = pltpu.make_async_remote_copy(
            src_ref=src, dst_ref=dst, send_sem=send_sem, recv_sem=recv_sem,
            device_id=device, device_id_type=MESH,
        )
        copy.start()
        return copy

    def dp_spread(phase, src_of, dst):
        def step(i, carry):
            peer = dp_peer(15 - i)
            remote(src_of(peer), dst, dp_send.at[phase], dp_recv.at[phase], (peer, s))
            return carry

        lax.fori_loop(0, 15, step, 0)

    def sh_spread(phase, src_of, dst):
        def step(i, carry):
            peer = sh_peer(31 - i)
            remote(src_of(peer), dst, sh_send.at[phase], sh_recv.at[phase], (d, peer))
            return carry

        lax.fori_loop(0, 31, step, 0)

    def wait_bytes(ref, sem):
        pltpu.make_async_copy(ref, ref, sem).wait()

    a_copies = []
    for n, k in enumerate((2, 1, 3, 0)):
        xd = lax.rem(x + k, 4)
        a_copies.append(
            remote(
                g_ref.at[:, xd, 1 - core], buf_a.at[:, xd], a_send.at[n], a_recv.at[n],
                (d + 1 - 2 * core, s),
            )
        )

    tok = owner_ref[...] * 256 + row_ref[...]
    tok_tile = jnp.broadcast_to(tok, (8, 128))
    tok_mine[...] = tok_tile
    tok_all[s] = tok_tile
    sh_spread(0, lambda peer: tok_mine, tok_all.at[s])

    load_own.wait()

    def add_pair(zi, xd):
        own[zi, xd] = (own[zi, xd].astype(F32) + buf_a[zi, xd].astype(F32)).astype(BF16)

    x1, x2, x3 = lax.rem(x + 1, 4), lax.rem(x + 2, 4), lax.rem(x + 3, 4)
    a_copies[0].wait_recv()
    for zi in range(2):
        add_pair(zi, x2)
    b1 = []
    for p, (r0, n) in enumerate(PIECES):
        for zi, k in ((0, 1), (1, 3)):
            b1.append(
                remote(
                    own.at[zi, x2, pl.ds(r0, n)], buf_b1.at[zi, pl.ds(r0, n)],
                    b1_send.at[p, zi], b1_recv.at[p, zi], x_dev(k),
                )
            )
    a_copies[1].wait_recv()
    a_copies[2].wait_recv()
    add_pair(1, x1)
    add_pair(0, x3)
    b2 = {}
    for p, (r0, n) in enumerate(PIECES):
        for zi, xd, k in ((1, x1, 1), (0, x3, 3)):
            b2[p, zi, 0] = remote(
                own.at[zi, xd, pl.ds(r0, n)], buf_b2.at[zi, 0, pl.ds(r0, n)],
                b2_send.at[p, zi, 0], b2_recv.at[p, zi, 0], x_dev(k),
            )
    add_pair(0, x1)
    add_pair(1, x3)

    proj_all[pl.ds(pl.multiple_of(d * 16, 16), 16)] = proj_ref[
        :, pl.ds(pl.multiple_of(d * 256, 256), 256)
    ]
    dp_spread(
        0,
        lambda peer: proj_ref.at[:, pl.ds(pl.multiple_of(peer * 256, 256), 256)],
        proj_all.at[pl.ds(pl.multiple_of(d * 16, 16), 16)],
    )

    for p, (r0, n) in enumerate(PIECES):
        for zi, xd, k in ((0, x1, 1), (1, x3, 3)):
            b1[2 * p + zi].wait_recv()
            own[zi, xd, pl.ds(r0, n)] = (
                own[zi, xd, pl.ds(r0, n)].astype(F32) + buf_b1[zi, pl.ds(r0, n)].astype(F32)
            ).astype(BF16)
            b2[p, zi, 1] = remote(
                own.at[zi, xd, pl.ds(r0, n)], buf_b2.at[zi, 1, pl.ds(r0, n)],
                b2_send.at[p, zi, 1], b2_recv.at[p, zi, 1], x_dev(k),
            )
    a_copies[3].wait_recv()
    for zi in range(2):
        add_pair(zi, x)

    wait_bytes(tok_all.at[pl.ds(0, 31)], sh_recv.at[0])
    tokens = tok_all[:, 0, :]
    member = (tokens // 256) == s
    row_plus = (lax.rem(tokens, 256) + 1).astype(F32)
    before = (iota((128, 128), 0) < iota((128, 128), 1)).astype(F32).astype(BF16)
    rank = dot(member.astype(F32).astype(BF16), before)
    lane = iota((32, 128), 1)
    want = jnp.zeros((32, 128), F32)
    for k in range(8):
        chosen = jnp.where(member & (rank == float(k)), row_plus, 0.0)
        want = want + jnp.where(lane == k, jnp.sum(chosen, axis=1, keepdims=True), 0.0)
    line = iota((256, 32), 0)
    pick = iota((256, 32), 1) == lax.rem(line // 8, 2) * 16 + lax.rem(
        line // 16 + 16 - lax.rem(line, 8), 16
    )
    spread = dot(pick.astype(F32).astype(BF16), want.astype(BF16))
    spread = jnp.where(iota((256, 128), 1) == lax.rem(iota((256, 128), 0), 8), spread, 0.0)
    idx_send[...] = dot(spread.astype(BF16), jnp.ones((128, 128), BF16)).astype(BF16)
    mine16 = pl.ds(pl.multiple_of(d * 16, 16), 16)
    idx_all[mine16] = idx_send[mine16]
    dp_spread(
        1,
        lambda peer: idx_send.at[pl.ds(pl.multiple_of(peer * 16, 16), 16)],
        idx_all.at[mine16],
    )

    wait_bytes(proj_all.at[pl.ds(0, 240)], dp_recv.at[0])
    block = proj_all[...]
    scaled = block.astype(F32) * gain_ref[:, pl.ds(pl.multiple_of(d * 256, 256), 256)]
    high = scaled.astype(BF16)
    low = (scaled - high.astype(F32)).astype(BF16)
    weights = w_ref[...]
    folded = (dot_t(weights, high) + dot_t(weights, low)).astype(BF16)
    gram = dot_t(block, block).astype(BF16)
    for o in range(16):
        if o < 12:
            part_send[o, 0:16] = folded[16 * o : 16 * o + 16]
        else:
            part_send[o, 0:16] = jnp.zeros((16, 256), BF16)
        part_send[o, 16:32] = gram[16 * o : 16 * o + 16]
    part_all[d] = part_send[d]
    dp_spread(2, lambda peer: part_send.at[peer], part_all.at[d])

    c_copies = []
    for p, (r0, n) in enumerate(PIECES):
        for zi in range(2):
            b2[p, zi, 0].wait_recv()
            b2[p, zi, 1].wait_recv()

        def total_of(zi):
            return (
                own[zi, x, pl.ds(r0, n)].astype(F32)
                + buf_b2[zi, 0, pl.ds(r0, n)].astype(F32)
                + buf_b2[zi, 1, pl.ds(r0, n)].astype(F32)
            )

        send_c[pl.ds(r0, n)] = total_of(1 - zh).astype(BF16)
        c_copies.append(
            remote(
                send_c.at[pl.ds(r0, n)], buf_c.at[pl.ds(r0, n)], c_send.at[p], c_recv.at[p],
                (lax.rem(d + 8, 16), s),
            )
        )
        summed_ref[pl.ds(r0, n)] = total_of(zh)

    wait_bytes(part_all.at[pl.ds(0, 15)], dp_recv.at[2])
    whole = part_all[0].astype(F32)
    for o in range(1, 16):
        whole = whole + part_all[o].astype(F32)
    w_mine[...] = whole.astype(BF16)
    w_all[d] = whole.astype(BF16)
    dp_spread(3, lambda peer: w_mine, w_all.at[d])

    wait_bytes(idx_all.at[pl.ds(0, 240)], dp_recv.at[1])
    ids = idx_all[...].astype(F32)
    for half in range(2):
        at = (iota((256, 128), 1) + 1 + 128 * half).astype(F32)
        onehot[:, 128 * half : 128 * half + 128] = jnp.where(ids == at, 1.0, 0.0).astype(BF16)

    squares = jnp.zeros((8, 256), F32)
    for p, (r0, n) in enumerate(PIECES):
        c_copies[p].wait_recv()
        total = summed_ref[pl.ds(r0, n)] + buf_c[pl.ds(r0, n)].astype(F32)
        summed_ref[pl.ds(r0, n)] = total
        squares = squares + jnp.sum((total * total).reshape(n // 8, 8, 256), axis=0)
    tile = squares[:, :128] + squares[:, 128:]
    sq1_mine[...] = tile
    sq1_all[d] = tile
    dp_spread(4, lambda peer: sq1_mine, sq1_all.at[d])

    owner_row = (tok // 256).astype(F32)
    owner_line = jnp.broadcast_to(owner_row, (128, 128))
    owner_col = owner_line.T
    earlier = iota((128, 128), 1) < iota((128, 128), 0)
    slot = jnp.sum(jnp.where((owner_col == owner_line) & earlier, 1.0, 0.0), axis=1, keepdims=True)
    place = owner_col[:, 0:1] * 16.0 + slot
    at = iota((128, 512), 1).astype(F32)
    find_left = jnp.where(at == place, 1.0, 0.0).astype(BF16)
    find_right = jnp.where(at == place + 8.0, 1.0, 0.0).astype(BF16)

    wait_bytes(sq1_all.at[pl.ds(0, 15)], dp_recv.at[4])
    tile = jnp.sum(sq1_all[...], axis=0)
    sq2_mine[...] = tile
    sq2_all[s] = tile
    sh_spread(1, lambda peer: sq2_mine, sq2_all.at[s])

    line, col = iota((512, 256), 0), iota((512, 256), 1)
    to, unit = line // 16, lax.rem(line, 16)
    k = lax.rem(unit, 8)
    match = col == lax.rem(to + k, 16) * 16 + (to // 16) * 8 + k
    pack_left = jnp.where(match & (unit < 8), 1.0, 0.0).astype(BF16)
    pack_right = jnp.where(match & (unit >= 8), 1.0, 0.0).astype(BF16)
    for load in loads:
        load.wait()

    wait_bytes(sq2_all.at[pl.ds(0, 31)], sh_recv.at[1])
    total = jnp.sum(sq2_all[...], axis=0)
    total = jnp.sum(jnp.sum(total, axis=0, keepdims=True), axis=1, keepdims=True)
    clip = jnp.minimum(1.0, 0.2 * math.sqrt(TOTAL_ENTRIES) / (jnp.sqrt(total) + 1e-06))
    grad = clip * summed_ref[...]
    new_m1 = 0.9 * state[1] + 0.1 * grad
    new_m2 = 0.95 * state[2] + 0.05 * grad * grad
    one = new_m1 / (1.0 - 0.9**10)
    two = new_m2 / (1.0 - 0.95**10)
    master = state[0]
    new_master = master - 0.01 * (one / (jnp.sqrt(two) + 1e-08) + 0.1 * master)
    o_m1[...] = new_m1
    o_m2[...] = new_m2
    o_master[...] = new_master

    table = new_master.astype(BF16)
    found = dot(onehot[:, 0:ROWS], table).astype(BF16)
    rows_send[...] = found
    rows_all[mine16] = rows_send[mine16]
    dp_spread(
        5,
        lambda peer: rows_send.at[pl.ds(pl.multiple_of(peer * 16, 16), 16)],
        rows_all.at[mine16],
    )
    wait_bytes(rows_all.at[pl.ds(0, 240)], dp_recv.at[5])
    rows = rows_all[...]
    back_send[...] = (dot(pack_left, rows[:, :128]) + dot(pack_right, rows[:, 128:])).astype(BF16)
    mine_s = pl.ds(pl.multiple_of(s * 16, 16), 16)
    back_all[mine_s] = back_send[mine_s]
    sh_spread(
        2,
        lambda peer: back_send.at[pl.ds(pl.multiple_of(peer * 16, 16), 16)],
        back_all.at[mine_s],
    )
    wait_bytes(w_all.at[pl.ds(0, 15)], dp_recv.at[3])
    gram = w_all[:, 16:32, :].reshape(256, 256)
    folded = w_all[0:12, 0:16, :].reshape(192, 256)
    wait_bytes(back_all.at[pl.ds(0, 496)], sh_recv.at[2])
    back = back_all[...]
    rows = jnp.concatenate([dot(find_left, back), dot(find_right, back)], axis=1)
    mean_sq = jnp.sum(dot(rows.astype(BF16), gram) * rows, axis=1, keepdims=True) / 4096.0
    gathered[s] = (rows * lax.rsqrt(mean_sq + 1e-05)).astype(BF16)

    z_copies = []
    for k in range(1, 4):
        z_copies.append(
            remote(
                gathered.at[s], gathered.at[s], z_send.at[4 - k], z_recv.at[4 - k],
                (d, y * 4 + lax.rem(z + k, 4)),
            )
        )

    def project(at):
        o_q[:, pl.ds(pl.multiple_of(at * 128, 128), 128)] = dot_t(folded, gathered[at]).astype(BF16)

    def block_at(step, way, j):
        back_by = (8 - step) if way == 0 else step
        return lax.rem(y + back_by, 8) * 4 + lax.rem(z + j, 4)

    def ring_copy(step, way, j):
        at = block_at(step, way, j)
        return pltpu.make_async_remote_copy(
            src_ref=gathered.at[at], dst_ref=gathered.at[at],
            send_sem=y_send.at[way, step, j], recv_sem=y_recv.at[way, step, j],
            device_id=y_dev(1 if way == 0 else 7), device_id_type=MESH,
        )

    def arrived(step, way, j):
        at = block_at(step, way, j)
        pltpu.make_async_copy(gathered.at[at], gathered.at[at], y_recv.at[way, step - 1, j]).wait()

    for j in range(4):
        if j:
            at = y * 4 + lax.rem(z + j, 4)
            pltpu.make_async_copy(gathered.at[at], gathered.at[at], z_recv.at[j]).wait()
        ring_copy(0, 0, j).start()
        ring_copy(0, 1, j).start()
        project(block_at(0, 0, j))
    for step in (1, 2):
        for j in range(4):
            for way in range(2):
                arrived(step, way, j)
                ring_copy(step, way, j).start()
                project(block_at(step, way, j))
    for j in range(4):
        for way in range(2):
            arrived(3, way, j)
            if j // 2 == way:
                ring_copy(3, way, j).start()
            project(block_at(3, way, j))
    for j in range(4):
        arrived(4, j // 2, j)
        project(block_at(4, j // 2, j))

    for copy in a_copies + b1 + list(b2.values()) + c_copies + z_copies:
        copy.wait_send()
    for phase, ref in enumerate(
        (proj_all.at[pl.ds(0, 240)], idx_all.at[pl.ds(0, 240)], part_all.at[pl.ds(0, 15)],
         w_all.at[pl.ds(0, 15)], sq1_all.at[pl.ds(0, 15)], rows_all.at[pl.ds(0, 240)])
    ):
        wait_bytes(ref, dp_send.at[phase])
    for phase, ref in enumerate(
        (tok_all.at[pl.ds(0, 31)], sq2_all.at[pl.ds(0, 31)], back_all.at[pl.ds(0, 496)])
    ):
        wait_bytes(ref, sh_send.at[phase])
    for step in range(4):
        for j in range(4):
            for way in range(2):
                if step < 3 or j // 2 == way:
                    ring_copy(step, way, j).wait_send()


def body(grad_groups, master, moment1, moment2, proj, ln_gain, w_qkv, token_owner, token_row):
    vmem = pl.BlockSpec(memory_space=pltpu.VMEM)
    hbm = pl.BlockSpec(memory_space=pl.ANY)
    dma = pltpu.SemaphoreType.DMA
    new_master, new_m1, new_m2, qkv_t = pl.pallas_call(
        kernel,
        out_shape=(
            jax.ShapeDtypeStruct((ROWS, 256), F32),
            jax.ShapeDtypeStruct((ROWS, 256), F32),
            jax.ShapeDtypeStruct((ROWS, 256), F32),
            jax.ShapeDtypeStruct((192, 4096), BF16),
        ),
        in_specs=[hbm] * 4 + [vmem] * 5,
        out_specs=[vmem] * 4,
        scratch_shapes=[
            pltpu.VMEM((2, 4, ROWS, 256), BF16),
            pltpu.VMEM((2, 4, ROWS, 256), BF16),
            pltpu.VMEM((2, ROWS, 256), BF16),
            pltpu.VMEM((2, 2, ROWS, 256), BF16),
            pltpu.VMEM((ROWS, 256), BF16),
            pltpu.VMEM((ROWS, 256), BF16),
            pltpu.VMEM((3, ROWS, 256), F32),
            pltpu.VMEM((ROWS, 256), F32),
            pltpu.VMEM((8, 128), jnp.int32),
            pltpu.VMEM((32, 8, 128), jnp.int32),
            pltpu.VMEM((256, 128), BF16),
            pltpu.VMEM((256, 128), BF16),
            pltpu.VMEM((256, 256), BF16),
            pltpu.VMEM((256, 256), BF16),
            pltpu.VMEM((16, 32, 256), BF16),
            pltpu.VMEM((16, 32, 256), BF16),
            pltpu.VMEM((32, 256), BF16),
            pltpu.VMEM((16, 32, 256), BF16),
            pltpu.VMEM((8, 128), F32),
            pltpu.VMEM((16, 8, 128), F32),
            pltpu.VMEM((8, 128), F32),
            pltpu.VMEM((32, 8, 128), F32),
            pltpu.VMEM((256, 256), BF16),
            pltpu.VMEM((256, 256), BF16),
            pltpu.VMEM((512, 128), BF16),
            pltpu.VMEM((512, 128), BF16),
            pltpu.VMEM((32, 128, 256), BF16),
            dma((4,)),
            dma((4,)), dma((4,)),
            dma((2, 2)), dma((2, 2)),
            dma((2, 2, 2)), dma((2, 2, 2)),
            dma((2,)), dma((2,)),
            dma((6,)), dma((6,)),
            dma((3,)), dma((3,)),
            dma((4,)), dma((4,)),
            dma((2, 4, 4)), dma((2, 4, 4)),
        ],
        compiler_params=pltpu.CompilerParams(
            collective_id=0, has_side_effects=True, vmem_limit_bytes=40 << 20
        ),
        name="step",
    )(
        grad_groups.reshape(2, 4, 2, ROWS, 256),
        master,
        moment1,
        moment2,
        proj,
        ln_gain.reshape(1, 4096),
        w_qkv.T,
        token_owner.reshape(1, 128),
        token_row.reshape(1, 128),
    )
    return new_master, new_m1, new_m2, qkv_t.T


def solution(mesh):
    placed = (
        P("dp", "shard", None),
        P(("shard", "dp"), None),
        P(("shard", "dp"), None),
        P(("shard", "dp"), None),
        P("dp", None),
        P(),
        P("dp", "shard"),
        P(("dp", "shard"), None),
        P(("dp", "shard")),
    )
    return jax.shard_map(
        body,
        mesh=mesh,
        in_specs=placed,
        out_specs=(
            P(("shard", "dp"), None),
            P(("shard", "dp"), None),
            P(("shard", "dp"), None),
            P("dp", "shard"),
        ),
        check_vma=False,
    )
```

```python
import math

import jax
import jax.numpy as jnp
from jax import lax
from jax.experimental import pallas as pl
from jax.experimental.pallas import tpu as pltpu
from jax.sharding import PartitionSpec as P

MESH = pl.DeviceIdType.MESH
F32 = jnp.float32
BF16 = jnp.bfloat16
ROWS = 208
FIRST = 96
PIECES = ((0, 112), (112, 96))
TOTAL_ENTRIES = 106496 * 256


def dot(a, b):
    return lax.dot_general(a, b, (((1,), (0,)), ((), ())), preferred_element_type=F32)


def dot_t(a, b):
    return lax.dot_general(a, b, (((1,), (1,)), ((), ())), preferred_element_type=F32)


def iota(shape, axis):
    return lax.broadcasted_iota(jnp.int32, shape, axis)


def kernel(
    g_ref, master_ref, m1_ref, m2_ref, proj_hbm, gain_hbm, w_hbm, owner_hbm, row_hbm,
    o_master, o_m1, o_m2, o_q,
    proj_ref, gain_ref, w_ref, owner_ref, row_ref,
    own, buf_a, buf_b1, buf_b2, send_c, buf_c, state, summed_ref,
    tok_mine, tok_all, idx_send, idx_all, onehot, proj_all, part_send, part_all, w_mine, w_all,
    sq1_mine, sq1_all, sq2_mine, sq2_all, rows_send, rows_all, back_send, back_all, gathered, qkv,
    local_sem, out_sem, a_send, a_recv, b1_send, b1_recv, b2_send, b2_recv, c_send, c_recv,
    dp_send, dp_recv, sh_send, sh_recv, z_send, z_recv, y_send, y_recv, yl_send, yl_recv, zl_send, zl_recv,
):
    d = lax.axis_index("dp")
    s = lax.axis_index("shard")
    core, x, zh = lax.rem(d, 2), lax.rem(d // 2, 4), d // 8
    y, z = s // 4, lax.rem(s, 4)

    def dp_peer(i):
        kz, kx, kc = i // 8, lax.rem(i // 2, 4), lax.rem(i, 2)
        return lax.rem(zh + kz, 2) * 8 + lax.rem(x + kx, 4) * 2 + lax.rem(core + kc, 2)

    def sh_peer(i):
        return lax.rem(y + i // 4, 8) * 4 + lax.rem(z + lax.rem(i, 4), 4)

    def x_dev(k):
        return (zh * 8 + lax.rem(x + k, 4) * 2 + core, s)

    def y_dev(k):
        return (d, lax.rem(y + k, 8) * 4 + z)

    loads = []
    for n, (src, dst) in enumerate(
        (
            (owner_hbm, owner_ref), (row_hbm, row_ref), (g_ref.at[:, :, core], own),
            (proj_hbm, proj_ref), (w_hbm, w_ref), (gain_hbm, gain_ref),
            (master_ref, state.at[0]), (m1_ref, state.at[1]), (m2_ref, state.at[2]),
        )
    ):
        load = pltpu.make_async_copy(src, dst, local_sem.at[n])
        load.start()
        loads.append(load)

    barrier = pltpu.get_barrier_semaphore()

    def greet_dp(i, carry):
        pl.semaphore_signal(barrier, inc=1, device_id=(dp_peer(1 + i), s), device_id_type=MESH)
        return carry

    def greet_sh(i, carry):
        pl.semaphore_signal(barrier, inc=1, device_id=(d, sh_peer(1 + i)), device_id_type=MESH)
        return carry

    lax.fori_loop(0, 15, greet_dp, 0)
    lax.fori_loop(0, 31, greet_sh, 0)
    pl.semaphore_wait(barrier, 46)

    sent = []

    def copy_to(src, dst, send_sem, recv_sem, device):
        return pltpu.make_async_remote_copy(
            src_ref=src, dst_ref=dst, send_sem=send_sem, recv_sem=recv_sem,
            device_id=device, device_id_type=MESH,
        )

    def remote(src, dst, send_sem, recv_sem, device):
        copy = copy_to(src, dst, send_sem, recv_sem, device)
        copy.start()
        sent.append(copy.wait_send)
        return copy

    def dp_spread(phase, batch, src_of, dst):
        def step(i, carry):
            peer = dp_peer(15 - i)
            copy_to(src_of(peer), dst, dp_send.at[phase], dp_recv.at[phase], (peer, s)).start()
            return carry

        lax.fori_loop(0, 15, step, 0)
        sent.append(lambda: wait_bytes(batch, dp_send.at[phase]))
        return lambda: wait_bytes(batch, dp_recv.at[phase])

    def sh_spread(phase, batch, src_of, dst):
        def step(i, carry):
            peer = sh_peer(31 - i)
            copy_to(src_of(peer), dst, sh_send.at[phase], sh_recv.at[phase], (d, peer)).start()
            return carry

        lax.fori_loop(0, 31, step, 0)
        sent.append(lambda: wait_bytes(batch, sh_send.at[phase]))
        return lambda: wait_bytes(batch, sh_recv.at[phase])

    def wait_bytes(ref, sem):
        pltpu.make_async_copy(ref, ref, sem).wait()

    a_copies = []
    for n, k in enumerate((2, 1, 3, 0)):
        xd = lax.rem(x + k, 4)
        a_copies.append(
            remote(
                g_ref.at[:, xd, 1 - core], buf_a.at[:, xd], a_send.at[n], a_recv.at[n],
                (d + 1 - 2 * core, s),
            )
        )

    loads[2].wait()

    def add_pair(zi, xd):
        own[zi, xd] = (own[zi, xd].astype(F32) + buf_a[zi, xd].astype(F32)).astype(BF16)

    x1, x2, x3 = lax.rem(x + 1, 4), lax.rem(x + 2, 4), lax.rem(x + 3, 4)
    a_copies[0].wait_recv()
    for zi in range(2):
        add_pair(zi, x2)
    b1 = []
    for p, (r0, n) in enumerate(PIECES):
        for zi, k in ((0, 1), (1, 3)):
            b1.append(
                remote(
                    own.at[zi, x2, pl.ds(r0, n)], buf_b1.at[zi, pl.ds(r0, n)],
                    b1_send.at[p, zi], b1_recv.at[p, zi], x_dev(k),
                )
            )
    loads[0].wait()
    loads[1].wait()
    tok = owner_ref[...] * 256 + row_ref[...]
    tok_tile = jnp.broadcast_to(tok, (8, 128))
    tok_mine[...] = tok_tile
    tok_all[s] = tok_tile
    tokens_in = sh_spread(0, tok_all.at[pl.ds(0, 31)], lambda peer: tok_mine, tok_all.at[s])

    a_copies[1].wait_recv()
    a_copies[2].wait_recv()
    add_pair(1, x1)
    add_pair(0, x3)
    b2 = {}
    for p, (r0, n) in enumerate(PIECES):
        for zi, xd, k in ((1, x1, 1), (0, x3, 3)):
            b2[p, zi, 0] = remote(
                own.at[zi, xd, pl.ds(r0, n)], buf_b2.at[zi, 0, pl.ds(r0, n)],
                b2_send.at[p, zi, 0], b2_recv.at[p, zi, 0], x_dev(k),
            )
    add_pair(0, x1)
    add_pair(1, x3)

    for p, (r0, n) in enumerate(PIECES):
        for zi, xd, k in ((0, x1, 1), (1, x3, 3)):
            b1[2 * p + zi].wait_recv()
            own[zi, xd, pl.ds(r0, n)] = (
                own[zi, xd, pl.ds(r0, n)].astype(F32) + buf_b1[zi, pl.ds(r0, n)].astype(F32)
            ).astype(BF16)
            b2[p, zi, 1] = remote(
                own.at[zi, xd, pl.ds(r0, n)], buf_b2.at[zi, 1, pl.ds(r0, n)],
                b2_send.at[p, zi, 1], b2_recv.at[p, zi, 1], x_dev(k),
            )
    loads[3].wait()
    proj_all[pl.ds(pl.multiple_of(d * 16, 16), 16)] = proj_ref[
        :, pl.ds(pl.multiple_of(d * 256, 256), 256)
    ]
    proj_in = dp_spread(
        0,
        proj_all.at[pl.ds(0, 240)],
        lambda peer: proj_ref.at[:, pl.ds(pl.multiple_of(peer * 256, 256), 256)],
        proj_all.at[pl.ds(pl.multiple_of(d * 16, 16), 16)],
    )

    a_copies[3].wait_recv()
    for zi in range(2):
        add_pair(zi, x)

    tokens_in()
    tokens = tok_all[:, 0, :]
    member = (tokens >> 8) == s
    row_plus = ((tokens & 255) + 1).astype(F32)
    before = (iota((128, 128), 0) < iota((128, 128), 1)).astype(F32).astype(BF16)
    rank = dot(member.astype(F32).astype(BF16), before)
    lane = iota((32, 128), 1)
    want = jnp.zeros((32, 128), F32)
    for k in range(8):
        chosen = jnp.where(member & (rank == float(k)), row_plus, 0.0)
        want = want + jnp.where(lane == k, jnp.sum(chosen, axis=1, keepdims=True), 0.0)
    line = iota((256, 32), 0)
    pick = iota((256, 32), 1) == ((line >> 3) & 1) * 16 + (((line >> 4) - (line & 7)) & 15)
    spread = dot(pick.astype(F32).astype(BF16), want.astype(BF16))
    spread = jnp.where(iota((256, 128), 1) == (iota((256, 128), 0) & 7), spread, 0.0)
    idx_send[...] = dot(spread.astype(BF16), jnp.ones((128, 128), BF16)).astype(BF16)
    mine16 = pl.ds(pl.multiple_of(d * 16, 16), 16)
    idx_all[mine16] = idx_send[mine16]
    idx_in = dp_spread(
        1,
        idx_all.at[pl.ds(0, 240)],
        lambda peer: idx_send.at[pl.ds(pl.multiple_of(peer * 16, 16), 16)],
        idx_all.at[mine16],
    )

    c_copies = []
    for p, (r0, n) in enumerate(PIECES):
        for zi in range(2):
            b2[p, zi, 0].wait_recv()
            b2[p, zi, 1].wait_recv()

        def total_of(zi):
            return (
                own[zi, x, pl.ds(r0, n)].astype(F32)
                + buf_b2[zi, 0, pl.ds(r0, n)].astype(F32)
                + buf_b2[zi, 1, pl.ds(r0, n)].astype(F32)
            )

        send_c[pl.ds(r0, n)] = total_of(1 - zh).astype(BF16)
        c_copies.append(
            remote(
                send_c.at[pl.ds(r0, n)], buf_c.at[pl.ds(r0, n)], c_send.at[p], c_recv.at[p],
                (lax.rem(d + 8, 16), s),
            )
        )
        summed_ref[pl.ds(r0, n)] = total_of(zh)

    proj_in()
    loads[4].wait()
    loads[5].wait()
    block = proj_all[...]
    scaled = block.astype(F32) * gain_ref[:, pl.ds(pl.multiple_of(d * 256, 256), 256)]
    high = scaled.astype(BF16)
    low = (scaled - high.astype(F32)).astype(BF16)
    weights = w_ref[...]
    folded = (dot_t(weights, high) + dot_t(weights, low)).astype(BF16)
    gram = dot_t(block, block).astype(BF16)
    for o in range(16):
        if o < 12:
            part_send[o, 0:16] = folded[16 * o : 16 * o + 16]
        else:
            part_send[o, 0:16] = jnp.zeros((16, 256), BF16)
        part_send[o, 16:32] = gram[16 * o : 16 * o + 16]
    part_all[d] = part_send[d]
    idx_in()
    ids = idx_all[...].astype(F32)
    for half in range(2):
        at = (iota((256, 128), 1) + 1 + 128 * half).astype(F32)
        onehot[:, 128 * half : 128 * half + 128] = jnp.where(ids == at, 1.0, 0.0).astype(BF16)

    squares = jnp.zeros((8, 256), F32)
    for p, (r0, n) in enumerate(PIECES):
        c_copies[p].wait_recv()
        total = summed_ref[pl.ds(r0, n)] + buf_c[pl.ds(r0, n)].astype(F32)
        summed_ref[pl.ds(r0, n)] = total
        squares = squares + jnp.sum((total * total).reshape(n // 8, 8, 256), axis=0)
    tile = squares[:, :128] + squares[:, 128:]
    sq1_mine[...] = tile
    sq1_all[d] = tile
    sq1_in = dp_spread(4, sq1_all.at[pl.ds(0, 15)], lambda peer: sq1_mine, sq1_all.at[d])

    part_in = dp_spread(2, part_all.at[pl.ds(0, 15)], lambda peer: part_send.at[peer], part_all.at[d])

    owner_row = (tok >> 8).astype(F32)
    owner_line = jnp.broadcast_to(owner_row, (128, 128))
    owner_col = owner_line.T
    earlier = iota((128, 128), 1) < iota((128, 128), 0)
    slot = jnp.sum(jnp.where((owner_col == owner_line) & earlier, 1.0, 0.0), axis=1, keepdims=True)
    place = owner_col[:, 0:1] * 16.0 + slot
    at = iota((128, 512), 1).astype(F32)
    find_left = jnp.where(at == place, 1.0, 0.0).astype(BF16)
    find_right = jnp.where(at == place + 8.0, 1.0, 0.0).astype(BF16)

    sq1_in()
    tile = jnp.sum(sq1_all[...], axis=0)
    sq2_mine[...] = tile
    sq2_all[s] = tile
    sq2_in = sh_spread(1, sq2_all.at[pl.ds(0, 31)], lambda peer: sq2_mine, sq2_all.at[s])

    line, col = iota((512, 256), 0), iota((512, 256), 1)
    to, unit = line >> 4, line & 15
    k = unit & 7
    match = col == ((to + k) & 15) * 16 + (to >> 4) * 8 + k
    pack_left = jnp.where(match & (unit < 8), 1.0, 0.0).astype(BF16)
    pack_right = jnp.where(match & (unit >= 8), 1.0, 0.0).astype(BF16)
    part_in()
    whole = part_all[0].astype(F32)
    for o in range(1, 16):
        whole = whole + part_all[o].astype(F32)
    w_mine[...] = whole.astype(BF16)
    w_all[d] = whole.astype(BF16)
    weights_in = dp_spread(3, w_all.at[pl.ds(0, 15)], lambda peer: w_mine, w_all.at[d])

    for load in loads[6:]:
        load.wait()

    sq2_in()
    total = jnp.sum(sq2_all[...], axis=0)
    total = jnp.sum(jnp.sum(total, axis=0, keepdims=True), axis=1, keepdims=True)
    clip = jnp.minimum(1.0, 0.2 * math.sqrt(TOTAL_ENTRIES) / (jnp.sqrt(total) + 1e-06))
    grad = clip * summed_ref[...]
    new_m1 = 0.9 * state[1] + 0.1 * grad
    new_m2 = 0.95 * state[2] + 0.05 * grad * grad
    one = new_m1 / (1.0 - 0.9**10)
    two = new_m2 / (1.0 - 0.95**10)
    master = state[0]
    new_master = master - 0.01 * (one / (jnp.sqrt(two) + 1e-08) + 0.1 * master)
    table = new_master.astype(BF16)
    found = dot(onehot[:, 0:ROWS], table).astype(BF16)
    rows_send[...] = found
    rows_all[mine16] = rows_send[mine16]
    rows_in = dp_spread(
        5,
        rows_all.at[pl.ds(0, 240)],
        lambda peer: rows_send.at[pl.ds(pl.multiple_of(peer * 16, 16), 16)],
        rows_all.at[mine16],
    )
    state[0] = new_master
    state[1] = new_m1
    state[2] = new_m2
    for n, ref in enumerate((o_master, o_m1, o_m2)):
        store = pltpu.make_async_copy(state.at[n], ref, out_sem.at[n])
        store.start()
        sent.append(store.wait)
    rows_in()
    rows = rows_all[...]
    back_send[...] = (dot(pack_left, rows[:, :128]) + dot(pack_right, rows[:, 128:])).astype(BF16)
    mine_s = pl.ds(pl.multiple_of(s * 16, 16), 16)
    back_all[mine_s] = back_send[mine_s]
    back_in = sh_spread(
        2,
        back_all.at[pl.ds(0, 496)],
        lambda peer: back_send.at[pl.ds(pl.multiple_of(peer * 16, 16), 16)],
        back_all.at[mine_s],
    )
    weights_in()
    gram = w_all[:, 16:32, :].reshape(256, 256)
    folded = w_all[0:12, 0:16, :].reshape(192, 256)
    back_in()
    back = back_all[...]
    rows = jnp.concatenate([dot(find_left, back), dot(find_right, back)], axis=1)
    mean_sq = jnp.sum(dot(rows.astype(BF16), gram) * rows, axis=1, keepdims=True) / 4096.0
    gathered[s] = (rows * lax.rsqrt(mean_sq + 1e-05)).astype(BF16)

    first, last = pl.ds(0, FIRST), pl.ds(FIRST, 128 - FIRST)

    def block_at(step, way, j):
        back_by = (8 - step) if way == 0 else step
        return lax.rem(y + back_by, 8) * 4 + lax.rem(z + j, 4)

    def ring_to(way):
        return y_dev(1 if way == 0 else 7)

    def first_on(step, way, j):
        part = gathered.at[block_at(step, way, j), first]
        remote(part, part, y_send.at[way, step, j], y_recv.at[way, step, j], ring_to(way))

    def first_in(step, way, j):
        part = gathered.at[block_at(step, way, j), first]
        wait_bytes(part, y_recv.at[way, step - 1, j])

    def last_rows(step, way):
        if step < 3:
            return last
        half = (128 - FIRST) // 2
        return pl.ds(FIRST + way * half, half)

    def last_on(step, way):
        part = gathered.at[block_at(step, way, 0), last_rows(step, way)]
        remote(part, part, yl_send.at[way, step], yl_recv.at[way, step], ring_to(way))

    def last_in(step, way):
        part = gathered.at[block_at(step, way, 0), last_rows(step - 1, way)]
        wait_bytes(part, yl_recv.at[way, step - 1])

    def last_along_z(step, way):
        part = gathered.at[block_at(step, way, 0), last]
        for k in (2, 1, 3):
            remote(
                part, part, zl_send.at[way, step - 1, 4 - k], zl_recv.at[way, step - 1, 4 - k],
                (d, y * 4 + lax.rem(z + k, 4)),
            )

    def project(step, way, j):
        at = block_at(step, way, j)
        if step and j:
            wait_bytes(gathered.at[at, last], zl_recv.at[way, step - 1, j])
        columns = pl.ds(pl.multiple_of(at * 128, 128), 128)
        qkv[:, columns] = dot_t(folded, gathered[at]).astype(BF16)
        pltpu.make_async_copy(qkv.at[:, columns], o_q.at[:, columns], out_sem.at[3]).start()

    for way in range(2):
        last_on(0, way)
    for k in (2, 1, 3):
        remote(
            gathered.at[s], gathered.at[s], z_send.at[4 - k], z_recv.at[4 - k],
            (d, y * 4 + lax.rem(z + k, 4)),
        )
    for j in range(4):
        if j:
            wait_bytes(gathered.at[block_at(0, 0, j)], z_recv.at[j])
        for way in range(2):
            first_on(0, way, j)
        project(0, 0, j)
    for step in (1, 2, 3):
        for way in range(2):
            last_in(step, way)
            last_on(step, way)
            last_along_z(step, way)
        for j in range(4):
            for way in range(2):
                first_in(step, way, j)
                if step < 3 or j // 2 == way:
                    first_on(step, way, j)
        if step > 1:
            for j in range(4):
                for way in range(2):
                    project(step - 1, way, j)
    for way in range(2):
        last_in(4, way)
    last_along_z(4, 0)
    for j in range(4):
        for way in range(2):
            project(3, way, j)
    for j in range(4):
        first_in(4, j // 2, j)
        project(4, 0, j)

    wait_bytes(qkv, out_sem.at[3])
    for wait in sent:
        wait()


def store_kernel(*refs):
    sources, targets, held, sem = refs[:4], refs[4:8], refs[8:12], refs[12]
    parts = [(n, slice(None)) for n in range(3)] + [(3, pl.ds(1024 * c, 1024)) for c in range(4)]
    loads = [
        pltpu.make_async_copy(sources[n].at[:, at], held[n].at[:, at], sem.at[0, i])
        for i, (n, at) in enumerate(parts)
    ]
    stores = [
        pltpu.make_async_copy(held[n].at[:, at], targets[n].at[:, at], sem.at[1, i])
        for i, (n, at) in enumerate(parts)
    ]
    for load in loads:
        load.start()
    for load, store in zip(loads, stores):
        load.wait()
        store.start()
    for store in stores:
        store.wait()


def body(grad_groups, master, moment1, moment2, proj, ln_gain, w_qkv, token_owner, token_row):
    hbm = pl.BlockSpec(memory_space=pltpu.HBM)
    dma = pltpu.SemaphoreType.DMA
    results = pl.pallas_call(
        kernel,
        out_shape=(
            jax.ShapeDtypeStruct((ROWS, 256), F32),
            jax.ShapeDtypeStruct((ROWS, 256), F32),
            jax.ShapeDtypeStruct((ROWS, 256), F32),
            jax.ShapeDtypeStruct((192, 4096), BF16),
        ),
        in_specs=[hbm] * 9,
        out_specs=[hbm] * 4,
        scratch_shapes=[
            pltpu.VMEM((16, 4096), BF16),
            pltpu.VMEM((1, 4096), F32),
            pltpu.VMEM((192, 256), BF16),
            pltpu.VMEM((1, 128), jnp.int32),
            pltpu.VMEM((1, 128), jnp.int32),
            pltpu.VMEM((2, 4, ROWS, 256), BF16),
            pltpu.VMEM((2, 4, ROWS, 256), BF16),
            pltpu.VMEM((2, ROWS, 256), BF16),
            pltpu.VMEM((2, 2, ROWS, 256), BF16),
            pltpu.VMEM((ROWS, 256), BF16),
            pltpu.VMEM((ROWS, 256), BF16),
            pltpu.VMEM((3, ROWS, 256), F32),
            pltpu.VMEM((ROWS, 256), F32),
            pltpu.VMEM((8, 128), jnp.int32),
            pltpu.VMEM((32, 8, 128), jnp.int32),
            pltpu.VMEM((256, 128), BF16),
            pltpu.VMEM((256, 128), BF16),
            pltpu.VMEM((256, 256), BF16),
            pltpu.VMEM((256, 256), BF16),
            pltpu.VMEM((16, 32, 256), BF16),
            pltpu.VMEM((16, 32, 256), BF16),
            pltpu.VMEM((32, 256), BF16),
            pltpu.VMEM((16, 32, 256), BF16),
            pltpu.VMEM((8, 128), F32),
            pltpu.VMEM((16, 8, 128), F32),
            pltpu.VMEM((8, 128), F32),
            pltpu.VMEM((32, 8, 128), F32),
            pltpu.VMEM((256, 256), BF16),
            pltpu.VMEM((256, 256), BF16),
            pltpu.VMEM((512, 128), BF16),
            pltpu.VMEM((512, 128), BF16),
            pltpu.VMEM((32, 128, 256), BF16),
            pltpu.VMEM((192, 4096), BF16),
            dma((9,)),
            dma((4,)),
            dma((4,)), dma((4,)),
            dma((2, 2)), dma((2, 2)),
            dma((2, 2, 2)), dma((2, 2, 2)),
            dma((2,)), dma((2,)),
            dma((6,)), dma((6,)),
            dma((3,)), dma((3,)),
            dma((4,)), dma((4,)),
            dma((2, 4, 4)), dma((2, 4, 4)),
            dma((2, 4)), dma((2, 4)),
            dma((2, 4, 4)), dma((2, 4, 4)),
        ],
        compiler_params=pltpu.CompilerParams(
            collective_id=0, has_side_effects=True, vmem_limit_bytes=56 << 20
        ),
        name="step",
    )(
        grad_groups.reshape(2, 4, 2, ROWS, 256),
        master,
        moment1,
        moment2,
        proj,
        ln_gain.reshape(1, 4096),
        w_qkv.T,
        token_owner.reshape(1, 128),
        token_row.reshape(1, 128),
    )
    new_master, new_m1, new_m2, qkv_t = pl.pallas_call(
        store_kernel,
        out_shape=tuple(jax.ShapeDtypeStruct(a.shape, a.dtype) for a in results),
        in_specs=[pl.BlockSpec(memory_space=pl.ANY)] * 4,
        out_specs=[hbm] * 4,
        scratch_shapes=[pltpu.VMEM(a.shape, a.dtype) for a in results] + [dma((2, 7))],
        name="store",
    )(*results)
    return new_master, new_m1, new_m2, qkv_t.T


def solution(mesh):
    placed = (
        P("dp", "shard", None),
        P(("shard", "dp"), None),
        P(("shard", "dp"), None),
        P(("shard", "dp"), None),
        P("dp", None),
        P(),
        P("dp", "shard"),
        P(("dp", "shard"), None),
        P(("dp", "shard")),
    )
    return jax.shard_map(
        body,
        mesh=mesh,
        in_specs=placed,
        out_specs=(
            P(("shard", "dp"), None),
            P(("shard", "dp"), None),
            P(("shard", "dp"), None),
            P("dp", "shard"),
        ),
        check_vma=False,
    )
```

```python
import math

import jax
import jax.numpy as jnp
from jax import lax
from jax.experimental import pallas as pl
from jax.experimental.pallas import tpu as pltpu
from jax.sharding import PartitionSpec as P

MESH = pl.DeviceIdType.MESH
F32 = jnp.float32
BF16 = jnp.bfloat16
ROWS = 208
FIRST = 96
PIECES = ((0, 112), (112, 96))
TOTAL_ENTRIES = 106496 * 256


def dot(a, b):
    return lax.dot_general(a, b, (((1,), (0,)), ((), ())), preferred_element_type=F32)


def dot_t(a, b):
    return lax.dot_general(a, b, (((1,), (1,)), ((), ())), preferred_element_type=F32)


def iota(shape, axis):
    return lax.broadcasted_iota(jnp.int32, shape, axis)


def kernel(
    g_ref, master_ref, m1_ref, m2_ref, proj_hbm, gain_hbm, w_hbm, owner_hbm, row_hbm,
    o_master, o_m1, o_m2, o_q,
    proj_ref, gain_ref, w_ref, owner_ref, row_ref,
    own, buf_a, buf_b1, buf_b2, send_c, buf_c, state, summed_ref,
    tok_mine, tok_all, idx_send, idx_all, onehot, proj_all, part_send, part_a, part_sum, part_b, w_pair, w_all,
    sq_mine, sq_all, rows_send, rows_all, back_send, back_all, gathered, qkv,
    local_sem, out_sem, a_send, a_recv, b1_send, b1_recv, b2_send, b2_recv, c_send, c_recv,
    dp_send, dp_recv, sh_send, sh_recv, few_send, few_recv, w_send, w_recv, z_send, z_recv, y_send, y_recv, yl_send, yl_recv, zl_send, zl_recv,
):
    d = lax.axis_index("dp")
    s = lax.axis_index("shard")
    core, x, zh = lax.rem(d, 2), lax.rem(d // 2, 4), d // 8
    y, z = s // 4, lax.rem(s, 4)

    def dp_peer(i):
        kz, kx, kc = i // 8, lax.rem(i // 2, 4), lax.rem(i, 2)
        return lax.rem(zh + kz, 2) * 8 + lax.rem(x + kx, 4) * 2 + lax.rem(core + kc, 2)

    def sh_peer(i):
        return lax.rem(y + i // 4, 8) * 4 + lax.rem(z + lax.rem(i, 4), 4)

    def far_dev(i):
        at = lax.rem(zh * 4 + z + i, 8)
        return ((at // 4) * 8 + lax.rem(d, 8), y * 4 + lax.rem(at, 4))

    def x_dev(k):
        return (zh * 8 + lax.rem(x + k, 4) * 2 + core, s)

    def y_dev(k):
        return (d, lax.rem(y + k, 8) * 4 + z)

    loads = []
    for n, (src, dst) in enumerate(
        (
            (owner_hbm, owner_ref), (row_hbm, row_ref), (g_ref.at[:, :, core], own),
            (proj_hbm, proj_ref), (w_hbm, w_ref), (gain_hbm, gain_ref),
            (master_ref, state.at[0]), (m1_ref, state.at[1]), (m2_ref, state.at[2]),
        )
    ):
        load = pltpu.make_async_copy(src, dst, local_sem.at[n])
        load.start()
        loads.append(load)

    barrier = pltpu.get_barrier_semaphore()

    def greet_dp(i, carry):
        pl.semaphore_signal(barrier, inc=1, device_id=(dp_peer(1 + i), s), device_id_type=MESH)
        return carry

    def greet_sh(i, carry):
        pl.semaphore_signal(barrier, inc=1, device_id=(d, sh_peer(1 + i)), device_id_type=MESH)
        return carry

    for i in (1, 2, 3, 5, 6, 7):

        @pl.when(lax.rem(z + i, 8) >= 4)
        def _():
            pl.semaphore_signal(barrier, inc=1, device_id=far_dev(i), device_id_type=MESH)

    lax.fori_loop(0, 15, greet_dp, 0)
    lax.fori_loop(0, 31, greet_sh, 0)
    pl.semaphore_wait(barrier, 49)

    sent = []

    def copy_to(src, dst, send_sem, recv_sem, device):
        return pltpu.make_async_remote_copy(
            src_ref=src, dst_ref=dst, send_sem=send_sem, recv_sem=recv_sem,
            device_id=device, device_id_type=MESH,
        )

    def remote(src, dst, send_sem, recv_sem, device):
        copy = copy_to(src, dst, send_sem, recv_sem, device)
        copy.start()
        sent.append(copy.wait_send)
        return copy

    def dp_spread(phase, batch, src_of, dst):
        def step(i, carry):
            peer = dp_peer(15 - i)
            copy_to(src_of(peer), dst, dp_send.at[phase], dp_recv.at[phase], (peer, s)).start()
            return carry

        lax.fori_loop(0, 15, step, 0)
        sent.append(lambda: wait_bytes(batch, dp_send.at[phase]))
        return lambda: wait_bytes(batch, dp_recv.at[phase])

    def sh_spread(phase, batch, src_of, dst):
        def step(i, carry):
            peer = sh_peer(31 - i)
            copy_to(src_of(peer), dst, sh_send.at[phase], sh_recv.at[phase], (d, peer)).start()
            return carry

        lax.fori_loop(0, 31, step, 0)
        sent.append(lambda: wait_bytes(batch, sh_send.at[phase]))
        return lambda: wait_bytes(batch, sh_recv.at[phase])

    def few_spread(phase, batch, src_of, dst, device_of):
        for i in range(7, 0, -1):
            copy_to(src_of(i), dst, few_send.at[phase], few_recv.at[phase], device_of(i)).start()
        sent.append(lambda: wait_bytes(batch, few_send.at[phase]))
        return lambda: wait_bytes(batch, few_recv.at[phase])

    def chip_dev(i):
        return (dp_peer(i), s)

    def wait_bytes(ref, sem):
        pltpu.make_async_copy(ref, ref, sem).wait()

    a_copies = []
    for n, k in enumerate((2, 1, 3, 0)):
        xd = lax.rem(x + k, 4)
        a_copies.append(
            remote(
                g_ref.at[:, xd, 1 - core], buf_a.at[:, xd], a_send.at[n], a_recv.at[n],
                (d + 1 - 2 * core, s),
            )
        )

    loads[2].wait()

    def add_pair(zi, xd):
        own[zi, xd] = (own[zi, xd].astype(F32) + buf_a[zi, xd].astype(F32)).astype(BF16)

    x1, x2, x3 = lax.rem(x + 1, 4), lax.rem(x + 2, 4), lax.rem(x + 3, 4)
    a_copies[0].wait_recv()
    for zi in range(2):
        add_pair(zi, x2)
    b1 = []
    for p, (r0, n) in enumerate(PIECES):
        for zi, k in ((0, 1), (1, 3)):
            b1.append(
                remote(
                    own.at[zi, x2, pl.ds(r0, n)], buf_b1.at[zi, pl.ds(r0, n)],
                    b1_send.at[p, zi], b1_recv.at[p, zi], x_dev(k),
                )
            )
    loads[0].wait()
    loads[1].wait()
    tok = owner_ref[...] * 256 + row_ref[...]
    tok_tile = jnp.broadcast_to(tok, (8, 128))
    tok_mine[...] = tok_tile
    tok_all[s] = tok_tile
    tokens_in = sh_spread(0, tok_all.at[pl.ds(0, 31)], lambda peer: tok_mine, tok_all.at[s])

    a_copies[1].wait_recv()
    a_copies[2].wait_recv()
    add_pair(1, x1)
    add_pair(0, x3)
    b2 = {}
    for p, (r0, n) in enumerate(PIECES):
        for zi, xd, k in ((1, x1, 1), (0, x3, 3)):
            b2[p, zi, 0] = remote(
                own.at[zi, xd, pl.ds(r0, n)], buf_b2.at[zi, 0, pl.ds(r0, n)],
                b2_send.at[p, zi, 0], b2_recv.at[p, zi, 0], x_dev(k),
            )
    add_pair(0, x1)
    add_pair(1, x3)

    for p, (r0, n) in enumerate(PIECES):
        for zi, xd, k in ((0, x1, 1), (1, x3, 3)):
            b1[2 * p + zi].wait_recv()
            own[zi, xd, pl.ds(r0, n)] = (
                own[zi, xd, pl.ds(r0, n)].astype(F32) + buf_b1[zi, pl.ds(r0, n)].astype(F32)
            ).astype(BF16)
            b2[p, zi, 1] = remote(
                own.at[zi, xd, pl.ds(r0, n)], buf_b2.at[zi, 1, pl.ds(r0, n)],
                b2_send.at[p, zi, 1], b2_recv.at[p, zi, 1], x_dev(k),
            )
    loads[3].wait()
    proj_all[pl.ds(pl.multiple_of(d * 16, 16), 16)] = proj_ref[
        :, pl.ds(pl.multiple_of(d * 256, 256), 256)
    ]
    proj_in = dp_spread(
        0,
        proj_all.at[pl.ds(0, 240)],
        lambda peer: proj_ref.at[:, pl.ds(pl.multiple_of(peer * 256, 256), 256)],
        proj_all.at[pl.ds(pl.multiple_of(d * 16, 16), 16)],
    )

    a_copies[3].wait_recv()
    for zi in range(2):
        add_pair(zi, x)

    tokens_in()
    tokens = tok_all[:, 0, :]
    member = (tokens >> 8) == s
    row_plus = ((tokens & 255) + 1).astype(F32)
    before = (iota((128, 128), 0) < iota((128, 128), 1)).astype(F32).astype(BF16)
    rank = dot(member.astype(F32).astype(BF16), before)
    lane = iota((32, 128), 1)
    want = jnp.zeros((32, 128), F32)
    for k in range(8):
        chosen = jnp.where(member & (rank == float(k)), row_plus, 0.0)
        want = want + jnp.where(lane == k, jnp.sum(chosen, axis=1, keepdims=True), 0.0)
    line = iota((256, 32), 0)
    pick = iota((256, 32), 1) == ((line >> 3) & 1) * 16 + (((line >> 4) - (line & 7)) & 15)
    spread = dot(pick.astype(F32).astype(BF16), want.astype(BF16))
    spread = jnp.where(iota((256, 128), 1) == (iota((256, 128), 0) & 7), spread, 0.0)
    idx_send[...] = dot(spread.astype(BF16), jnp.ones((128, 128), BF16)).astype(BF16)
    mine16 = pl.ds(pl.multiple_of(d * 16, 16), 16)
    idx_all[mine16] = idx_send[mine16]
    idx_in = dp_spread(
        1,
        idx_all.at[pl.ds(0, 240)],
        lambda peer: idx_send.at[pl.ds(pl.multiple_of(peer * 16, 16), 16)],
        idx_all.at[mine16],
    )

    c_copies = []
    for p, (r0, n) in enumerate(PIECES):
        for zi in range(2):
            b2[p, zi, 0].wait_recv()
            b2[p, zi, 1].wait_recv()

        def total_of(zi):
            return (
                own[zi, x, pl.ds(r0, n)].astype(F32)
                + buf_b2[zi, 0, pl.ds(r0, n)].astype(F32)
                + buf_b2[zi, 1, pl.ds(r0, n)].astype(F32)
            )

        send_c[pl.ds(r0, n)] = total_of(1 - zh).astype(BF16)
        c_copies.append(
            remote(
                send_c.at[pl.ds(r0, n)], buf_c.at[pl.ds(r0, n)], c_send.at[p], c_recv.at[p],
                (lax.rem(d + 8, 16), s),
            )
        )
        summed_ref[pl.ds(r0, n)] = total_of(zh)

    proj_in()
    loads[4].wait()
    loads[5].wait()
    block = proj_all[...]
    scaled = block.astype(F32) * gain_ref[:, pl.ds(pl.multiple_of(d * 256, 256), 256)]
    high = scaled.astype(BF16)
    low = (scaled - high.astype(F32)).astype(BF16)
    weights = w_ref[...]
    folded = (dot_t(weights, high) + dot_t(weights, low)).astype(BF16)
    gram = dot_t(block, block).astype(BF16)
    for o in range(16):
        if o < 12:
            part_send[o // 8, o % 8, 0:16] = folded[16 * o : 16 * o + 16]
        else:
            part_send[o // 8, o % 8, 0:16] = jnp.zeros((16, 256), BF16)
        part_send[o // 8, o % 8, 16:32] = gram[16 * o : 16 * o + 16]
    place8 = lax.rem(d, 8)
    part_a[place8] = part_send[:, place8]
    part_in = few_spread(
        0, part_a.at[pl.ds(0, 7)], lambda i: part_send.at[:, lax.rem(dp_peer(i), 8)],
        part_a.at[place8], chip_dev,
    )
    idx_in()
    ids = idx_all[...].astype(F32)
    for half in range(2):
        at = (iota((256, 128), 1) + 1 + 128 * half).astype(F32)
        onehot[:, 128 * half : 128 * half + 128] = jnp.where(ids == at, 1.0, 0.0).astype(BF16)

    squares = jnp.zeros((8, 256), F32)
    for p, (r0, n) in enumerate(PIECES):
        c_copies[p].wait_recv()
        total = summed_ref[pl.ds(r0, n)] + buf_c[pl.ds(r0, n)].astype(F32)
        summed_ref[pl.ds(r0, n)] = total
        squares = squares + jnp.sum((total * total).reshape(n // 8, 8, 256), axis=0)
    tile = squares[:, :128] + squares[:, 128:]
    def share(n, place, tile, device_of):
        sq_mine[n] = tile
        sq_all[n, place] = tile
        arrive = few_spread(
            2 + n, sq_all.at[n, pl.ds(0, 7)], lambda i: sq_mine.at[n], sq_all.at[n, place],
            device_of,
        )

        def total():
            arrive()
            return jnp.sum(sq_all[n], axis=0)

        return total

    sq_sum = share(0, place8, tile, chip_dev)

    part_in()
    half_sum = part_a[0].astype(F32)
    for o in range(1, 8):
        half_sum = half_sum + part_a[o].astype(F32)
    part_sum[...] = half_sum.astype(BF16)
    other = (lax.rem(d + 8, 16), s)
    part_b_copy = remote(part_sum.at[1 - zh], part_b, w_send.at[0], w_recv.at[0], other)

    owner_row = (tok >> 8).astype(F32)
    owner_line = jnp.broadcast_to(owner_row, (128, 128))
    owner_col = owner_line.T
    earlier = iota((128, 128), 1) < iota((128, 128), 0)
    slot = jnp.sum(jnp.where((owner_col == owner_line) & earlier, 1.0, 0.0), axis=1, keepdims=True)
    place = owner_col[:, 0:1] * 16.0 + slot
    at = iota((128, 512), 1).astype(F32)
    find_left = jnp.where(at == place, 1.0, 0.0).astype(BF16)
    find_right = jnp.where(at == place + 8.0, 1.0, 0.0).astype(BF16)

    sq_sum = share(1, zh * 4 + z, sq_sum(), far_dev)

    line, col = iota((512, 256), 0), iota((512, 256), 1)
    to, unit = line >> 4, line & 15
    k = unit & 7
    match = col == ((to + k) & 15) * 16 + (to >> 4) * 8 + k
    pack_left = jnp.where(match & (unit < 8), 1.0, 0.0).astype(BF16)
    pack_right = jnp.where(match & (unit >= 8), 1.0, 0.0).astype(BF16)
    part_b_copy.wait_recv()
    w_pair[zh] = (part_sum[zh].astype(F32) + part_b[...].astype(F32)).astype(BF16)
    w_pair_copy = remote(w_pair.at[zh], w_pair.at[zh], w_send.at[1], w_recv.at[1], other)

    sq_sum = share(2, y, sq_sum(), y_dev)
    for load in loads[6:]:
        load.wait()

    total = sq_sum()
    total = jnp.sum(jnp.sum(total, axis=0, keepdims=True), axis=1, keepdims=True)
    clip = jnp.minimum(1.0, 0.2 * math.sqrt(TOTAL_ENTRIES) / (jnp.sqrt(total) + 1e-06))
    grad = clip * summed_ref[...]
    new_m1 = 0.9 * state[1] + 0.1 * grad
    new_m2 = 0.95 * state[2] + 0.05 * grad * grad
    one = new_m1 / (1.0 - 0.9**10)
    two = new_m2 / (1.0 - 0.95**10)
    master = state[0]
    new_master = master - 0.01 * (one / (jnp.sqrt(two) + 1e-08) + 0.1 * master)
    table = new_master.astype(BF16)
    found = dot(onehot[:, 0:ROWS], table).astype(BF16)
    rows_send[...] = found
    rows_all[mine16] = rows_send[mine16]
    rows_in = dp_spread(
        2,
        rows_all.at[pl.ds(0, 240)],
        lambda peer: rows_send.at[pl.ds(pl.multiple_of(peer * 16, 16), 16)],
        rows_all.at[mine16],
    )
    w_pair_copy.wait_recv()
    w_all[:, place8] = w_pair[...]
    weights_in = few_spread(
        1, w_all.at[:, pl.ds(0, 7)], lambda i: w_pair, w_all.at[:, place8], chip_dev
    )
    state[0] = new_master
    state[1] = new_m1
    state[2] = new_m2
    for n, ref in enumerate((o_master, o_m1, o_m2)):
        store = pltpu.make_async_copy(state.at[n], ref, out_sem.at[n])
        store.start()
        sent.append(store.wait)
    rows_in()
    rows = rows_all[...]
    back_send[...] = (dot(pack_left, rows[:, :128]) + dot(pack_right, rows[:, 128:])).astype(BF16)
    mine_s = pl.ds(pl.multiple_of(s * 16, 16), 16)
    back_all[mine_s] = back_send[mine_s]
    back_in = sh_spread(
        1,
        back_all.at[pl.ds(0, 496)],
        lambda peer: back_send.at[pl.ds(pl.multiple_of(peer * 16, 16), 16)],
        back_all.at[mine_s],
    )
    weights_in()
    gram = w_all[:, :, 16:32, :].reshape(256, 256)
    folded = w_all[:, :, 0:16, :].reshape(256, 256)[0:192]
    back_in()
    back = back_all[...]
    rows = jnp.concatenate([dot(find_left, back), dot(find_right, back)], axis=1)
    mean_sq = jnp.sum(dot(rows.astype(BF16), gram) * rows, axis=1, keepdims=True) / 4096.0
    gathered[s] = (rows * lax.rsqrt(mean_sq + 1e-05)).astype(BF16)

    first, last = pl.ds(0, FIRST), pl.ds(FIRST, 128 - FIRST)
    z_order = (1, 3, 2)

    def z_of(j):
        return (z, z + 1 - 2 * lax.rem(z, 2), lax.rem(z + 2, 4), 3 - z)[j]

    def block_at(step, way, j):
        back_by = (8 - step) if way == 0 else step
        return lax.rem(y + back_by, 8) * 4 + z_of(j)

    def ring_to(way):
        return y_dev(1 if way == 0 else 7)

    def first_on(step, way, j):
        part = gathered.at[block_at(step, way, j), first]
        remote(part, part, y_send.at[way, step, j], y_recv.at[way, step, j], ring_to(way))

    def first_in(step, way, j):
        part = gathered.at[block_at(step, way, j), first]
        wait_bytes(part, y_recv.at[way, step - 1, j])

    def last_rows(step, way):
        if step < 3:
            return last
        half = (128 - FIRST) // 2
        return pl.ds(FIRST + way * half, half)

    def last_on(step, way):
        part = gathered.at[block_at(step, way, 0), last_rows(step, way)]
        remote(part, part, yl_send.at[way, step], yl_recv.at[way, step], ring_to(way))

    def last_in(step, way):
        part = gathered.at[block_at(step, way, 0), last_rows(step - 1, way)]
        wait_bytes(part, yl_recv.at[way, step - 1])

    def last_along_z(step, way):
        part = gathered.at[block_at(step, way, 0), last]
        for j in z_order:
            remote(
                part, part, zl_send.at[way, step - 1, j], zl_recv.at[way, step - 1, j],
                (d, y * 4 + z_of(j)),
            )

    def project(step, way, j):
        at = block_at(step, way, j)
        if step and j:
            wait_bytes(gathered.at[at, last], zl_recv.at[way, step - 1, j])
        columns = pl.ds(pl.multiple_of(at * 128, 128), 128)
        qkv[:, columns] = dot_t(folded, gathered[at]).astype(BF16)
        pltpu.make_async_copy(qkv.at[:, columns], o_q.at[:, columns], out_sem.at[3]).start()

    def own_along_z(rows, n):
        part = gathered.at[s, rows]
        for j in z_order:
            remote(part, part, z_send.at[n, j], z_recv.at[n, j], (d, y * 4 + z_of(j)))

    own_along_z(first, 0)
    for way in range(2):
        first_on(0, way, 0)
    for way in range(2):
        last_on(0, way)
    own_along_z(last, 1)
    project(0, 0, 0)
    for j in z_order:
        wait_bytes(gathered.at[block_at(0, 0, j), first], z_recv.at[0, j])
        for way in range(2):
            first_on(0, way, j)
    for j in z_order:
        wait_bytes(gathered.at[block_at(0, 0, j), last], z_recv.at[1, j])
        project(0, 0, j)
    for step in (1, 2, 3):
        for way in range(2):
            last_in(step, way)
            last_on(step, way)
            last_along_z(step, way)
        for j in (0,) + z_order:
            for way in range(2):
                first_in(step, way, j)
                if step < 3 or j // 2 == way:
                    first_on(step, way, j)
        if step > 1:
            for j in range(4):
                for way in range(2):
                    project(step - 1, way, j)
    for way in range(2):
        last_in(4, way)
    last_along_z(4, 0)
    for j in range(4):
        for way in range(2):
            project(3, way, j)
    for j in (0, 3, 1, 2):
        first_in(4, j // 2, j)
        project(4, 0, j)

    wait_bytes(qkv, out_sem.at[3])
    for wait in sent:
        wait()


def store_kernel(*refs):
    sources, targets, held, sem = refs[:4], refs[4:8], refs[8:12], refs[12]
    parts = [(n, slice(None)) for n in range(3)] + [(3, pl.ds(1024 * c, 1024)) for c in range(4)]
    loads = [
        pltpu.make_async_copy(sources[n].at[:, at], held[n].at[:, at], sem.at[0, i])
        for i, (n, at) in enumerate(parts)
    ]
    stores = [
        pltpu.make_async_copy(held[n].at[:, at], targets[n].at[:, at], sem.at[1, i])
        for i, (n, at) in enumerate(parts)
    ]
    for load in loads:
        load.start()
    for load, store in zip(loads, stores):
        load.wait()
        store.start()
    for store in stores:
        store.wait()


def body(grad_groups, master, moment1, moment2, proj, ln_gain, w_qkv, token_owner, token_row):
    hbm = pl.BlockSpec(memory_space=pltpu.HBM)
    dma = pltpu.SemaphoreType.DMA
    results = pl.pallas_call(
        kernel,
        out_shape=(
            jax.ShapeDtypeStruct((ROWS, 256), F32),
            jax.ShapeDtypeStruct((ROWS, 256), F32),
            jax.ShapeDtypeStruct((ROWS, 256), F32),
            jax.ShapeDtypeStruct((192, 4096), BF16),
        ),
        in_specs=[hbm] * 9,
        out_specs=[hbm] * 4,
        scratch_shapes=[
            pltpu.VMEM((16, 4096), BF16),
            pltpu.VMEM((1, 4096), F32),
            pltpu.VMEM((192, 256), BF16),
            pltpu.VMEM((1, 128), jnp.int32),
            pltpu.VMEM((1, 128), jnp.int32),
            pltpu.VMEM((2, 4, ROWS, 256), BF16),
            pltpu.VMEM((2, 4, ROWS, 256), BF16),
            pltpu.VMEM((2, ROWS, 256), BF16),
            pltpu.VMEM((2, 2, ROWS, 256), BF16),
            pltpu.VMEM((ROWS, 256), BF16),
            pltpu.VMEM((ROWS, 256), BF16),
            pltpu.VMEM((3, ROWS, 256), F32),
            pltpu.VMEM((ROWS, 256), F32),
            pltpu.VMEM((8, 128), jnp.int32),
            pltpu.VMEM((32, 8, 128), jnp.int32),
            pltpu.VMEM((256, 128), BF16),
            pltpu.VMEM((256, 128), BF16),
            pltpu.VMEM((256, 256), BF16),
            pltpu.VMEM((256, 256), BF16),
            pltpu.VMEM((2, 8, 32, 256), BF16),
            pltpu.VMEM((8, 2, 32, 256), BF16),
            pltpu.VMEM((2, 32, 256), BF16),
            pltpu.VMEM((32, 256), BF16),
            pltpu.VMEM((2, 32, 256), BF16),
            pltpu.VMEM((2, 8, 32, 256), BF16),
            pltpu.VMEM((3, 8, 128), F32),
            pltpu.VMEM((3, 8, 8, 128), F32),
            pltpu.VMEM((256, 256), BF16),
            pltpu.VMEM((256, 256), BF16),
            pltpu.VMEM((512, 128), BF16),
            pltpu.VMEM((512, 128), BF16),
            pltpu.VMEM((32, 128, 256), BF16),
            pltpu.VMEM((192, 4096), BF16),
            dma((9,)),
            dma((4,)),
            dma((4,)), dma((4,)),
            dma((2, 2)), dma((2, 2)),
            dma((2, 2, 2)), dma((2, 2, 2)),
            dma((2,)), dma((2,)),
            dma((3,)), dma((3,)),
            dma((2,)), dma((2,)),
            dma((5,)), dma((5,)),
            dma((2,)), dma((2,)),
            dma((2, 4)), dma((2, 4)),
            dma((2, 4, 4)), dma((2, 4, 4)),
            dma((2, 4)), dma((2, 4)),
            dma((2, 4, 4)), dma((2, 4, 4)),
        ],
        compiler_params=pltpu.CompilerParams(
            collective_id=0, has_side_effects=True, vmem_limit_bytes=56 << 20
        ),
        name="step",
    )(
        grad_groups.reshape(2, 4, 2, ROWS, 256),
        master,
        moment1,
        moment2,
        proj,
        ln_gain.reshape(1, 4096),
        w_qkv.T,
        token_owner.reshape(1, 128),
        token_row.reshape(1, 128),
    )
    new_master, new_m1, new_m2, qkv_t = pl.pallas_call(
        store_kernel,
        out_shape=tuple(jax.ShapeDtypeStruct(a.shape, a.dtype) for a in results),
        in_specs=[pl.BlockSpec(memory_space=pl.ANY)] * 4,
        out_specs=[hbm] * 4,
        scratch_shapes=[pltpu.VMEM(a.shape, a.dtype) for a in results] + [dma((2, 7))],
        name="store",
    )(*results)
    return new_master, new_m1, new_m2, qkv_t.T


def solution(mesh):
    placed = (
        P("dp", "shard", None),
        P(("shard", "dp"), None),
        P(("shard", "dp"), None),
        P(("shard", "dp"), None),
        P("dp", None),
        P(),
        P("dp", "shard"),
        P(("dp", "shard"), None),
        P(("dp", "shard")),
    )
    return jax.shard_map(
        body,
        mesh=mesh,
        in_specs=placed,
        out_specs=(
            P(("shard", "dp"), None),
            P(("shard", "dp"), None),
            P(("shard", "dp"), None),
            P("dp", "shard"),
        ),
        check_vma=False,
    )
```

```python
import math

import jax
import jax.numpy as jnp
from jax import lax
from jax.experimental import pallas as pl
from jax.experimental.pallas import tpu as pltpu
from jax.sharding import PartitionSpec as P

MESH = pl.DeviceIdType.MESH
F32 = jnp.float32
BF16 = jnp.bfloat16
ROWS = 208
FIRST = 96
FAR_FIRST = sorted(range(1, 32), key=lambda i: -min(i // 4, 8 - i // 4) - (i % 4 > 0))
PIECES = ((0, 112), (112, 96))
TOTAL_ENTRIES = 106496 * 256


def dot(a, b):
    return lax.dot_general(a, b, (((1,), (0,)), ((), ())), preferred_element_type=F32)


def dot_t(a, b):
    return lax.dot_general(a, b, (((1,), (1,)), ((), ())), preferred_element_type=F32)


def iota(shape, axis):
    return lax.broadcasted_iota(jnp.int32, shape, axis)


def kernel(
    g_ref, master_ref, m1_ref, m2_ref, proj_hbm, gain_hbm, w_hbm, owner_hbm, row_hbm,
    o_master, o_m1, o_m2, o_q,
    proj_ref, gain_ref, w_ref, owner_ref, row_ref,
    own, buf_a, buf_b1, buf_b2, send_c, buf_c, state, summed_ref,
    tok_all, idx_send, idx_all, onehot, proj_half, proj_all, part_send, part_a, part_sum, part_b, w_pair, w_all,
    sq_mine, sq_all, rows_send, rows_all, back_send, back_all, gathered, qkv,
    local_sem, out_sem, a_send, a_recv, b1_send, b1_recv, b2_send, b2_recv, c_send, c_recv,
    dp_send, dp_recv, sh_send, sh_recv, few_send, few_recv, w_send, w_recv,
    tz_send, tz_recv, ty_send, ty_recv, ph_send, ph_recv, z_send, z_recv, y_send, y_recv, yl_send, yl_recv, zl_send, zl_recv,
):
    d = lax.axis_index("dp")
    s = lax.axis_index("shard")
    core, x, zh = lax.rem(d, 2), lax.rem(d // 2, 4), d // 8
    y, z = s // 4, lax.rem(s, 4)

    def dp_peer(i):
        kz, kx, kc = i // 8, lax.rem(i // 2, 4), lax.rem(i, 2)
        return lax.rem(zh + kz, 2) * 8 + lax.rem(x + kx, 4) * 2 + lax.rem(core + kc, 2)

    def sh_peer(i):
        return lax.rem(y + i // 4, 8) * 4 + lax.rem(z + lax.rem(i, 4), 4)

    def far_dev(i):
        at = lax.rem(zh * 4 + z + i, 8)
        return ((at // 4) * 8 + lax.rem(d, 8), y * 4 + lax.rem(at, 4))

    def x_dev(k):
        return (zh * 8 + lax.rem(x + k, 4) * 2 + core, s)

    def y_dev(k):
        return (d, lax.rem(y + k, 8) * 4 + z)

    loads = []
    for n, (src, dst) in enumerate(
        (
            (owner_hbm, owner_ref), (row_hbm, row_ref), (g_ref.at[:, :, core], own),
            (proj_hbm, proj_ref), (w_hbm, w_ref), (gain_hbm, gain_ref),
            (master_ref, state.at[0]), (m1_ref, state.at[1]), (m2_ref, state.at[2]),
        )
    ):
        load = pltpu.make_async_copy(src, dst, local_sem.at[n])
        load.start()
        loads.append(load)

    def z_of(j):
        return (z, z + 1 - 2 * lax.rem(z, 2), lax.rem(z + 2, 4), 3 - z)[j]

    z_order = (1, 3, 2)
    half_dev = (lax.rem(d + 8, 16), s)

    def line_dev(j):
        return (d, y * 4 + z_of(j))

    barrier = pltpu.get_barrier_semaphore()
    first_devs = [(d + 1 - 2 * core, s), x_dev(1), x_dev(3), half_dev, y_dev(1), y_dev(7)]
    first_devs += [line_dev(j) for j in z_order]
    for dev in first_devs:
        pl.semaphore_signal(barrier, inc=1, device_id=dev, device_id_type=MESH)
    pl.semaphore_wait(barrier, len(first_devs))

    sent = []

    def copy_to(src, dst, send_sem, recv_sem, device):
        return pltpu.make_async_remote_copy(
            src_ref=src, dst_ref=dst, send_sem=send_sem, recv_sem=recv_sem,
            device_id=device, device_id_type=MESH,
        )

    def remote(src, dst, send_sem, recv_sem, device):
        copy = copy_to(src, dst, send_sem, recv_sem, device)
        copy.start()
        sent.append(copy.wait_send)
        return copy

    def dp_spread(phase, batch, src_of, dst):
        for i in range(15, 0, -1):
            peer = dp_peer(i)
            copy_to(src_of(peer), dst, dp_send.at[phase], dp_recv.at[phase], (peer, s)).start()
        sent.append(lambda: wait_bytes(batch, dp_send.at[phase]))
        return lambda: wait_bytes(batch, dp_recv.at[phase])

    def sh_spread(phase, batch, src_of, dst):
        for i in FAR_FIRST:
            peer = sh_peer(i)
            copy_to(src_of(peer), dst, sh_send.at[phase], sh_recv.at[phase], (d, peer)).start()
        sent.append(lambda: wait_bytes(batch, sh_send.at[phase]))
        return lambda: wait_bytes(batch, sh_recv.at[phase])

    def few_spread(phase, batch, src_of, dst, device_of):
        for i in range(7, 0, -1):
            copy_to(src_of(i), dst, few_send.at[phase], few_recv.at[phase], device_of(i)).start()
        sent.append(lambda: wait_bytes(batch, few_send.at[phase]))
        return lambda: wait_bytes(batch, few_recv.at[phase])

    def chip_dev(i):
        return (dp_peer(i), s)

    def wait_bytes(ref, sem):
        pltpu.make_async_copy(ref, ref, sem).wait()

    a_copies = []
    for n, k in enumerate((2, 1, 3, 0)):
        xd = lax.rem(x + k, 4)
        a_copies.append(
            remote(
                g_ref.at[:, xd, 1 - core], buf_a.at[:, xd], a_send.at[n], a_recv.at[n],
                (d + 1 - 2 * core, s),
            )
        )

    loads[0].wait()
    loads[1].wait()
    tok = owner_ref[...] * 256 + row_ref[...]
    tok_all[s] = jnp.broadcast_to(tok, (8, 128))
    tok_z = [
        remote(tok_all.at[s], tok_all.at[s], tz_send.at[j], tz_recv.at[j], line_dev(j))
        for j in z_order
    ]

    def tok_set(step, way):
        return tok_all.at[pl.ds(lax.rem(y + ((8 - step) if way == 0 else step), 8) * 4, 4)]

    def tok_on(step, way):
        part = tok_set(step, way)
        remote(part, part, ty_send.at[way, step], ty_recv.at[way, step], y_dev(1 if way == 0 else 7))

    def tok_in(step, way):
        wait_bytes(tok_set(step, way), ty_recv.at[way, step - 1])

    loads[3].wait()
    half_columns = [pl.ds(pl.multiple_of(h * 2048, 2048), 2048) for h in (zh, 1 - zh)]
    proj_half_copy = remote(
        proj_ref.at[:, half_columns[1]], proj_half.at[zh], ph_send.at[0], ph_recv.at[0], half_dev
    )
    proj_half[zh] = proj_ref[:, half_columns[0]]

    loads[2].wait()

    def add_pair(zi, xd):
        own[zi, xd] = (own[zi, xd].astype(F32) + buf_a[zi, xd].astype(F32)).astype(BF16)

    x1, x2, x3 = lax.rem(x + 1, 4), lax.rem(x + 2, 4), lax.rem(x + 3, 4)
    a_copies[0].wait_recv()
    for zi in range(2):
        add_pair(zi, x2)
    b1 = []
    for p, (r0, n) in enumerate(PIECES):
        for zi, k in ((0, 1), (1, 3)):
            b1.append(
                remote(
                    own.at[zi, x2, pl.ds(r0, n)], buf_b1.at[zi, pl.ds(r0, n)],
                    b1_send.at[p, zi], b1_recv.at[p, zi], x_dev(k),
                )
            )
    a_copies[1].wait_recv()
    a_copies[2].wait_recv()
    add_pair(1, x1)
    add_pair(0, x3)
    b2 = {}
    for p, (r0, n) in enumerate(PIECES):
        for zi, xd, k in ((1, x1, 1), (0, x3, 3)):
            b2[p, zi, 0] = remote(
                own.at[zi, xd, pl.ds(r0, n)], buf_b2.at[zi, 0, pl.ds(r0, n)],
                b2_send.at[p, zi, 0], b2_recv.at[p, zi, 0], x_dev(k),
            )
    add_pair(0, x1)
    add_pair(1, x3)

    for copy in tok_z:
        copy.wait_recv()
    for way in range(2):
        tok_on(0, way)
    for p, (r0, n) in enumerate(PIECES):
        for zi, xd, k in ((0, x1, 1), (1, x3, 3)):
            b1[2 * p + zi].wait_recv()
            own[zi, xd, pl.ds(r0, n)] = (
                own[zi, xd, pl.ds(r0, n)].astype(F32) + buf_b1[zi, pl.ds(r0, n)].astype(F32)
            ).astype(BF16)
            b2[p, zi, 1] = remote(
                own.at[zi, xd, pl.ds(r0, n)], buf_b2.at[zi, 1, pl.ds(r0, n)],
                b2_send.at[p, zi, 1], b2_recv.at[p, zi, 1], x_dev(k),
            )
    for way in range(2):
        tok_in(1, way)
        tok_on(1, way)
    a_copies[3].wait_recv()
    for zi in range(2):
        add_pair(zi, x)

    c_copies = []
    for p, (r0, n) in enumerate(PIECES):
        for zi in range(2):
            b2[p, zi, 0].wait_recv()
            b2[p, zi, 1].wait_recv()

        def total_of(zi):
            return (
                own[zi, x, pl.ds(r0, n)].astype(F32)
                + buf_b2[zi, 0, pl.ds(r0, n)].astype(F32)
                + buf_b2[zi, 1, pl.ds(r0, n)].astype(F32)
            )

        send_c[pl.ds(r0, n)] = total_of(1 - zh).astype(BF16)
        c_copies.append(
            remote(
                send_c.at[pl.ds(r0, n)], buf_c.at[pl.ds(r0, n)], c_send.at[p], c_recv.at[p],
                (lax.rem(d + 8, 16), s),
            )
        )
        summed_ref[pl.ds(r0, n)] = total_of(zh)

    proj_half_copy.wait_recv()
    place8 = lax.rem(d, 8)

    def half_block(at):
        return proj_half.at[:, :, pl.ds(pl.multiple_of(at * 256, 256), 256)]

    proj_all[:, place8] = half_block(place8)[...]
    proj_in = few_spread(
        5, proj_all.at[:, pl.ds(0, 7)], lambda i: half_block(lax.rem(dp_peer(i), 8)),
        proj_all.at[:, place8], chip_dev,
    )
    for way in range(2):
        tok_in(2, way)
        tok_on(2, way)
    proj_in()
    loads[4].wait()
    loads[5].wait()
    block = proj_all[...].reshape(256, 256)
    scaled = block.astype(F32) * gain_ref[:, pl.ds(pl.multiple_of(d * 256, 256), 256)]
    high = scaled.astype(BF16)
    low = (scaled - high.astype(F32)).astype(BF16)
    weights = w_ref[...]
    folded = (dot_t(weights, high) + dot_t(weights, low)).astype(BF16)
    gram = dot_t(block, block).astype(BF16)
    for o in range(16):
        if o < 12:
            part_send[o // 8, o % 8, 0:16] = folded[16 * o : 16 * o + 16]
        else:
            part_send[o // 8, o % 8, 0:16] = jnp.zeros((16, 256), BF16)
        part_send[o // 8, o % 8, 16:32] = gram[16 * o : 16 * o + 16]
    part_a[place8] = part_send[:, place8]
    part_in = few_spread(
        0, part_a.at[pl.ds(0, 7)], lambda i: part_send.at[:, lax.rem(dp_peer(i), 8)],
        part_a.at[place8], chip_dev,
    )
    for way in range(2):
        tok_in(3, way)
    tok_on(3, 0)
    squares = jnp.zeros((8, 256), F32)
    for p, (r0, n) in enumerate(PIECES):
        c_copies[p].wait_recv()
        total = summed_ref[pl.ds(r0, n)] + buf_c[pl.ds(r0, n)].astype(F32)
        summed_ref[pl.ds(r0, n)] = total
        squares = squares + jnp.sum((total * total).reshape(n // 8, 8, 256), axis=0)
    tile = squares[:, :128] + squares[:, 128:]
    def share(n, place, tile, device_of):
        sq_mine[n] = tile
        sq_all[n, place] = tile
        arrive = few_spread(
            2 + n, sq_all.at[n, pl.ds(0, 7)], lambda i: sq_mine.at[n], sq_all.at[n, place],
            device_of,
        )

        def total():
            arrive()
            return jnp.sum(sq_all[n], axis=0)

        return total

    sq_sum = share(0, place8, tile, chip_dev)

    part_in()
    half_sum = part_a[0].astype(F32)
    for o in range(1, 8):
        half_sum = half_sum + part_a[o].astype(F32)
    part_sum[...] = half_sum.astype(BF16)
    part_b_copy = remote(part_sum.at[1 - zh], part_b, w_send.at[0], w_recv.at[0], half_dev)

    tok_in(4, 0)
    tokens = tok_all[:, 0, :]
    member = (tokens >> 8) == s
    row_plus = ((tokens & 255) + 1).astype(F32)
    before = (iota((128, 128), 0) < iota((128, 128), 1)).astype(F32).astype(BF16)
    rank = dot(member.astype(F32).astype(BF16), before)
    lane = iota((32, 128), 1)
    want = jnp.zeros((32, 128), F32)
    for k in range(8):
        chosen = jnp.where(member & (rank == float(k)), row_plus, 0.0)
        want = want + jnp.where(lane == k, jnp.sum(chosen, axis=1, keepdims=True), 0.0)
    line = iota((256, 32), 0)
    pick = iota((256, 32), 1) == ((line >> 3) & 1) * 16 + (((line >> 4) - (line & 7)) & 15)
    spread = dot(pick.astype(F32).astype(BF16), want.astype(BF16))
    spread = jnp.where(iota((256, 128), 1) == (iota((256, 128), 0) & 7), spread, 0.0)
    idx_send[...] = dot(spread.astype(BF16), jnp.ones((128, 128), BF16)).astype(BF16)
    mine16 = pl.ds(pl.multiple_of(d * 16, 16), 16)
    idx_all[mine16] = idx_send[mine16]
    idx_in = dp_spread(
        0,
        idx_all.at[pl.ds(0, 240)],
        lambda peer: idx_send.at[pl.ds(pl.multiple_of(peer * 16, 16), 16)],
        idx_all.at[mine16],
    )

    owner_row = (tok >> 8).astype(F32)
    owner_line = jnp.broadcast_to(owner_row, (128, 128))
    owner_col = owner_line.T
    earlier = iota((128, 128), 1) < iota((128, 128), 0)
    slot = jnp.sum(jnp.where((owner_col == owner_line) & earlier, 1.0, 0.0), axis=1, keepdims=True)
    place = owner_col[:, 0:1] * 16.0 + slot
    at = iota((128, 512), 1).astype(F32)
    find_left = jnp.where(at == place, 1.0, 0.0).astype(BF16)
    find_right = jnp.where(at == place + 8.0, 1.0, 0.0).astype(BF16)

    sq_sum = share(1, zh * 4 + z, sq_sum(), far_dev)

    line, col = iota((512, 256), 0), iota((512, 256), 1)
    to, unit = line >> 4, line & 15
    k = unit & 7
    match = col == ((to + k) & 15) * 16 + (to >> 4) * 8 + k
    pack_left = jnp.where(match & (unit < 8), 1.0, 0.0).astype(BF16)
    pack_right = jnp.where(match & (unit >= 8), 1.0, 0.0).astype(BF16)
    part_b_copy.wait_recv()
    w_pair[zh] = (part_sum[zh].astype(F32) + part_b[...].astype(F32)).astype(BF16)
    w_pair_copy = remote(w_pair.at[zh], w_pair.at[zh], w_send.at[1], w_recv.at[1], half_dev)

    sq_sum = share(2, y, sq_sum(), y_dev)
    idx_in()
    ids = idx_all[...].astype(F32)
    for half in range(2):
        at = (iota((256, 128), 1) + 1 + 128 * half).astype(F32)
        onehot[:, 128 * half : 128 * half + 128] = jnp.where(ids == at, 1.0, 0.0).astype(BF16)

    for load in loads[6:]:
        load.wait()

    total = sq_sum()
    total = jnp.sum(jnp.sum(total, axis=0, keepdims=True), axis=1, keepdims=True)
    clip = jnp.minimum(1.0, 0.2 * math.sqrt(TOTAL_ENTRIES) / (jnp.sqrt(total) + 1e-06))
    grad = clip * summed_ref[...]
    new_m1 = 0.9 * state[1] + 0.1 * grad
    new_m2 = 0.95 * state[2] + 0.05 * grad * grad
    one = new_m1 / (1.0 - 0.9**10)
    two = new_m2 / (1.0 - 0.95**10)
    master = state[0]
    new_master = master - 0.01 * (one / (jnp.sqrt(two) + 1e-08) + 0.1 * master)
    table = new_master.astype(BF16)
    found = dot(onehot[:, 0:ROWS], table).astype(BF16)
    rows_send[...] = found
    rows_all[mine16] = rows_send[mine16]
    rows_in = dp_spread(
        1,
        rows_all.at[pl.ds(0, 240)],
        lambda peer: rows_send.at[pl.ds(pl.multiple_of(peer * 16, 16), 16)],
        rows_all.at[mine16],
    )
    w_pair_copy.wait_recv()
    w_all[:, place8] = w_pair[...]
    weights_in = few_spread(
        1, w_all.at[:, pl.ds(0, 7)], lambda i: w_pair, w_all.at[:, place8], chip_dev
    )
    state[0] = new_master
    state[1] = new_m1
    state[2] = new_m2
    for n, ref in enumerate((o_master, o_m1, o_m2)):
        store = pltpu.make_async_copy(state.at[n], ref, out_sem.at[n])
        store.start()
        sent.append(store.wait)
    rows_in()
    rows = rows_all[...]
    back_send[...] = (dot(pack_left, rows[:, :128]) + dot(pack_right, rows[:, 128:])).astype(BF16)
    mine_s = pl.ds(pl.multiple_of(s * 16, 16), 16)
    back_all[mine_s] = back_send[mine_s]
    back_in = sh_spread(
        0,
        back_all.at[pl.ds(0, 496)],
        lambda peer: back_send.at[pl.ds(pl.multiple_of(peer * 16, 16), 16)],
        back_all.at[mine_s],
    )
    weights_in()
    gram = w_all[:, :, 16:32, :].reshape(256, 256)
    folded = w_all[:, :, 0:16, :].reshape(256, 256)[0:192]
    back_in()
    back = back_all[...]
    rows = jnp.concatenate([dot(find_left, back), dot(find_right, back)], axis=1)
    mean_sq = jnp.sum(dot(rows.astype(BF16), gram) * rows, axis=1, keepdims=True) / 4096.0
    gathered[s] = (rows * lax.rsqrt(mean_sq + 1e-05)).astype(BF16)

    first, last = pl.ds(0, FIRST), pl.ds(FIRST, 128 - FIRST)

    def block_at(step, way, j):
        back_by = (8 - step) if way == 0 else step
        return lax.rem(y + back_by, 8) * 4 + z_of(j)

    def ring_to(way):
        return y_dev(1 if way == 0 else 7)

    def first_on(step, way, j):
        part = gathered.at[block_at(step, way, j), first]
        remote(part, part, y_send.at[way, step, j], y_recv.at[way, step, j], ring_to(way))

    def first_in(step, way, j):
        part = gathered.at[block_at(step, way, j), first]
        wait_bytes(part, y_recv.at[way, step - 1, j])

    def last_rows(step, way):
        if step < 3:
            return last
        half = (128 - FIRST) // 2
        return pl.ds(FIRST + way * half, half)

    def last_on(step, way):
        part = gathered.at[block_at(step, way, 0), last_rows(step, way)]
        remote(part, part, yl_send.at[way, step], yl_recv.at[way, step], ring_to(way))

    def last_in(step, way):
        part = gathered.at[block_at(step, way, 0), last_rows(step - 1, way)]
        wait_bytes(part, yl_recv.at[way, step - 1])

    def last_along_z(step, way):
        part = gathered.at[block_at(step, way, 0), last]
        for j in z_order:
            remote(
                part, part, zl_send.at[way, step - 1, j], zl_recv.at[way, step - 1, j],
                (d, y * 4 + z_of(j)),
            )

    def project(step, way, j):
        at = block_at(step, way, j)
        if step and j:
            wait_bytes(gathered.at[at, last], zl_recv.at[way, step - 1, j])
        columns = pl.ds(pl.multiple_of(at * 128, 128), 128)
        qkv[:, columns] = dot_t(folded, gathered[at]).astype(BF16)
        pltpu.make_async_copy(qkv.at[:, columns], o_q.at[:, columns], out_sem.at[3]).start()

    def own_along_z(rows, n):
        part = gathered.at[s, rows]
        for j in z_order:
            remote(part, part, z_send.at[n, j], z_recv.at[n, j], (d, y * 4 + z_of(j)))

    own_along_z(first, 0)
    for way in range(2):
        first_on(0, way, 0)
    for way in range(2):
        last_on(0, way)
    own_along_z(last, 1)
    project(0, 0, 0)
    for j in z_order:
        wait_bytes(gathered.at[block_at(0, 0, j), first], z_recv.at[0, j])
        for way in range(2):
            first_on(0, way, j)
    for j in z_order:
        wait_bytes(gathered.at[block_at(0, 0, j), last], z_recv.at[1, j])
        project(0, 0, j)
    for step in (1, 2, 3):
        for way in range(2):
            last_in(step, way)
            last_on(step, way)
            last_along_z(step, way)
        for j in (0,) + z_order:
            for way in range(2):
                first_in(step, way, j)
                if step < 3 or j // 2 == way:
                    first_on(step, way, j)
        if step > 1:
            for j in range(4):
                for way in range(2):
                    project(step - 1, way, j)
    for way in range(2):
        last_in(4, way)
    last_along_z(4, 0)
    for j in range(4):
        for way in range(2):
            project(3, way, j)
    for j in (0, 3, 1, 2):
        first_in(4, j // 2, j)
        project(4, 0, j)

    wait_bytes(qkv, out_sem.at[3])
    for wait in sent:
        wait()


def store_kernel(*refs):
    sources, targets, held, sem = refs[:4], refs[4:8], refs[8:12], refs[12]
    parts = [(n, slice(None)) for n in range(3)] + [(3, pl.ds(1024 * c, 1024)) for c in range(4)]
    loads = [
        pltpu.make_async_copy(sources[n].at[:, at], held[n].at[:, at], sem.at[0, i])
        for i, (n, at) in enumerate(parts)
    ]
    stores = [
        pltpu.make_async_copy(held[n].at[:, at], targets[n].at[:, at], sem.at[1, i])
        for i, (n, at) in enumerate(parts)
    ]
    for load in loads:
        load.start()
    for load, store in zip(loads, stores):
        load.wait()
        store.start()
    for store in stores:
        store.wait()


def body(grad_groups, master, moment1, moment2, proj, ln_gain, w_qkv, token_owner, token_row):
    hbm = pl.BlockSpec(memory_space=pltpu.HBM)
    dma = pltpu.SemaphoreType.DMA
    results = pl.pallas_call(
        kernel,
        out_shape=(
            jax.ShapeDtypeStruct((ROWS, 256), F32),
            jax.ShapeDtypeStruct((ROWS, 256), F32),
            jax.ShapeDtypeStruct((ROWS, 256), F32),
            jax.ShapeDtypeStruct((192, 4096), BF16),
        ),
        in_specs=[hbm] * 9,
        out_specs=[hbm] * 4,
        scratch_shapes=[
            pltpu.VMEM((16, 4096), BF16),
            pltpu.VMEM((1, 4096), F32),
            pltpu.VMEM((192, 256), BF16),
            pltpu.VMEM((1, 128), jnp.int32),
            pltpu.VMEM((1, 128), jnp.int32),
            pltpu.VMEM((2, 4, ROWS, 256), BF16),
            pltpu.VMEM((2, 4, ROWS, 256), BF16),
            pltpu.VMEM((2, ROWS, 256), BF16),
            pltpu.VMEM((2, 2, ROWS, 256), BF16),
            pltpu.VMEM((ROWS, 256), BF16),
            pltpu.VMEM((ROWS, 256), BF16),
            pltpu.VMEM((3, ROWS, 256), F32),
            pltpu.VMEM((ROWS, 256), F32),
            pltpu.VMEM((32, 8, 128), jnp.int32),
            pltpu.VMEM((256, 128), BF16),
            pltpu.VMEM((256, 128), BF16),
            pltpu.VMEM((256, 256), BF16),
            pltpu.VMEM((2, 16, 2048), BF16),
            pltpu.VMEM((2, 8, 16, 256), BF16),
            pltpu.VMEM((2, 8, 32, 256), BF16),
            pltpu.VMEM((8, 2, 32, 256), BF16),
            pltpu.VMEM((2, 32, 256), BF16),
            pltpu.VMEM((32, 256), BF16),
            pltpu.VMEM((2, 32, 256), BF16),
            pltpu.VMEM((2, 8, 32, 256), BF16),
            pltpu.VMEM((3, 8, 128), F32),
            pltpu.VMEM((3, 8, 8, 128), F32),
            pltpu.VMEM((256, 256), BF16),
            pltpu.VMEM((256, 256), BF16),
            pltpu.VMEM((512, 128), BF16),
            pltpu.VMEM((512, 128), BF16),
            pltpu.VMEM((32, 128, 256), BF16),
            pltpu.VMEM((192, 4096), BF16),
            dma((9,)),
            dma((4,)),
            dma((4,)), dma((4,)),
            dma((len(PIECES), 2)), dma((len(PIECES), 2)),
            dma((len(PIECES), 2, 2)), dma((len(PIECES), 2, 2)),
            dma((len(PIECES),)), dma((len(PIECES),)),
            dma((2,)), dma((2,)),
            dma((1,)), dma((1,)),
            dma((6,)), dma((6,)),
            dma((2,)), dma((2,)),
            dma((4,)), dma((4,)),
            dma((2, 4)), dma((2, 4)),
            dma((1,)), dma((1,)),
            dma((2, 4)), dma((2, 4)),
            dma((2, 4, 4)), dma((2, 4, 4)),
            dma((2, 4)), dma((2, 4)),
            dma((2, 4, 4)), dma((2, 4, 4)),
        ],
        compiler_params=pltpu.CompilerParams(
            collective_id=0, has_side_effects=True, vmem_limit_bytes=56 << 20
        ),
        name="step",
    )(
        grad_groups.reshape(2, 4, 2, ROWS, 256),
        master,
        moment1,
        moment2,
        proj,
        ln_gain.reshape(1, 4096),
        w_qkv.T,
        token_owner.reshape(1, 128),
        token_row.reshape(1, 128),
    )
    new_master, new_m1, new_m2, qkv_t = pl.pallas_call(
        store_kernel,
        out_shape=tuple(jax.ShapeDtypeStruct(a.shape, a.dtype) for a in results),
        in_specs=[pl.BlockSpec(memory_space=pl.ANY)] * 4,
        out_specs=[hbm] * 4,
        scratch_shapes=[pltpu.VMEM(a.shape, a.dtype) for a in results] + [dma((2, 7))],
        name="store",
    )(*results)
    return new_master, new_m1, new_m2, qkv_t.T


def solution(mesh):
    placed = (
        P("dp", "shard", None),
        P(("shard", "dp"), None),
        P(("shard", "dp"), None),
        P(("shard", "dp"), None),
        P("dp", None),
        P(),
        P("dp", "shard"),
        P(("dp", "shard"), None),
        P(("dp", "shard")),
    )
    return jax.shard_map(
        body,
        mesh=mesh,
        in_specs=placed,
        out_specs=(
            P(("shard", "dp"), None),
            P(("shard", "dp"), None),
            P(("shard", "dp"), None),
            P("dp", "shard"),
        ),
        check_vma=False,
    )
```

```python
import math

import jax
import jax.numpy as jnp
from jax import lax
from jax.experimental import pallas as pl
from jax.experimental.pallas import tpu as pltpu
from jax.sharding import PartitionSpec as P

MESH = pl.DeviceIdType.MESH
F32 = jnp.float32
BF16 = jnp.bfloat16
ROWS = 208
FIRST = 80
FAR_FIRST = sorted(range(1, 32), key=lambda i: -min(i // 4, 8 - i // 4) - (i % 4 > 0))
PIECES = ((0, 112), (112, 96))
TOTAL_ENTRIES = 106496 * 256


def dot(a, b):
    return lax.dot_general(a, b, (((1,), (0,)), ((), ())), preferred_element_type=F32)


def dot_t(a, b):
    return lax.dot_general(a, b, (((1,), (1,)), ((), ())), preferred_element_type=F32)


def iota(shape, axis):
    return lax.broadcasted_iota(jnp.int32, shape, axis)


def kernel(
    g_ref, master_ref, m1_ref, m2_ref, proj_hbm, gain_hbm, w_hbm, owner_hbm, row_hbm,
    o_master, o_m1, o_m2, o_q,
    proj_ref, gain_ref, w_ref, owner_ref, row_ref,
    own, buf_a, buf_b1, buf_b2, send_c, buf_c, state, summed_ref,
    tok_all, idx_send, idx_all, onehot, proj_half, proj_all, part_send, part_a, part_sum, part_b, w_pair, w_all,
    sq_mine, sq_all, rows_send, rows_all, back_send, back_all, gathered, qkv,
    local_sem, out_sem, a_send, a_recv, b1_send, b1_recv, b2_send, b2_recv, c_send, c_recv,
    dp_send, dp_recv, sh_send, sh_recv, few_send, few_recv, w_send, w_recv,
    tz_send, tz_recv, ty_send, ty_recv, ph_send, ph_recv, z_send, z_recv, y_send, y_recv, yl_send, yl_recv, zl_send, zl_recv,
):
    d = lax.axis_index("dp")
    s = lax.axis_index("shard")
    core, x, zh = lax.rem(d, 2), lax.rem(d // 2, 4), d // 8
    y, z = s // 4, lax.rem(s, 4)

    def dp_peer(i):
        kz, kx, kc = i // 8, lax.rem(i // 2, 4), lax.rem(i, 2)
        return lax.rem(zh + kz, 2) * 8 + lax.rem(x + kx, 4) * 2 + lax.rem(core + kc, 2)

    def sh_peer(i):
        return lax.rem(y + i // 4, 8) * 4 + lax.rem(z + lax.rem(i, 4), 4)

    def far_dev(i):
        at = lax.rem(zh * 4 + z + i, 8)
        return ((at // 4) * 8 + lax.rem(d, 8), y * 4 + lax.rem(at, 4))

    def x_dev(k):
        return (zh * 8 + lax.rem(x + k, 4) * 2 + core, s)

    def y_dev(k):
        return (d, lax.rem(y + k, 8) * 4 + z)

    loads = []
    for n, (src, dst) in enumerate(
        (
            (owner_hbm, owner_ref), (row_hbm, row_ref), (g_ref.at[:, :, core], own),
            (proj_hbm, proj_ref), (w_hbm, w_ref), (gain_hbm, gain_ref),
            (master_ref, state.at[0]), (m1_ref, state.at[1]), (m2_ref, state.at[2]),
        )
    ):
        load = pltpu.make_async_copy(src, dst, local_sem.at[n])
        load.start()
        loads.append(load)

    def z_of(j):
        return (z, z + 1 - 2 * lax.rem(z, 2), lax.rem(z + 2, 4), 3 - z)[j]

    z_order = (1, 3, 2)
    half_dev = (lax.rem(d + 8, 16), s)

    def line_dev(j):
        return (d, y * 4 + z_of(j))

    barrier = pltpu.get_barrier_semaphore()
    first_devs = [(d + 1 - 2 * core, s), x_dev(1), x_dev(3), half_dev, y_dev(1), y_dev(7)]
    first_devs += [line_dev(j) for j in z_order]
    for dev in first_devs:
        pl.semaphore_signal(barrier, inc=1, device_id=dev, device_id_type=MESH)
    pl.semaphore_wait(barrier, len(first_devs))

    sent = []

    def settle(count):
        for wait in sent[:count]:
            wait()
        del sent[:count]


    def copy_to(src, dst, send_sem, recv_sem, device):
        return pltpu.make_async_remote_copy(
            src_ref=src, dst_ref=dst, send_sem=send_sem, recv_sem=recv_sem,
            device_id=device, device_id_type=MESH,
        )

    def remote(src, dst, send_sem, recv_sem, device):
        copy = copy_to(src, dst, send_sem, recv_sem, device)
        copy.start()
        sent.append(copy.wait_send)
        return copy

    def dp_spread(phase, batch, src_of, dst):
        for i in range(15, 0, -1):
            peer = dp_peer(i)
            copy_to(src_of(peer), dst, dp_send.at[phase], dp_recv.at[phase], (peer, s)).start()
        sent.append(lambda: wait_bytes(batch, dp_send.at[phase]))
        return lambda: wait_bytes(batch, dp_recv.at[phase])

    def sh_spread(phase, batch, src_of, dst):
        for i in FAR_FIRST:
            peer = sh_peer(i)
            copy_to(src_of(peer), dst, sh_send.at[phase], sh_recv.at[phase], (d, peer)).start()
        sent.append(lambda: wait_bytes(batch, sh_send.at[phase]))
        return lambda: wait_bytes(batch, sh_recv.at[phase])

    def few_spread(phase, batch, src_of, dst, device_of):
        for i in range(7, 0, -1):
            copy_to(src_of(i), dst, few_send.at[phase], few_recv.at[phase], device_of(i)).start()
        sent.append(lambda: wait_bytes(batch, few_send.at[phase]))
        return lambda: wait_bytes(batch, few_recv.at[phase])

    def chip_dev(i):
        return (dp_peer(i), s)

    def wait_bytes(ref, sem):
        pltpu.make_async_copy(ref, ref, sem).wait()

    a_copies = []
    for n, k in enumerate((2, 1, 3, 0)):
        xd = lax.rem(x + k, 4)
        a_copies.append(
            remote(
                g_ref.at[:, xd, 1 - core], buf_a.at[:, xd], a_send.at[n], a_recv.at[n],
                (d + 1 - 2 * core, s),
            )
        )

    loads[0].wait()
    loads[1].wait()
    tok = owner_ref[...] * 256 + row_ref[...]
    tok_all[s] = jnp.broadcast_to(tok, (8, 128))
    tok_z = [
        remote(tok_all.at[s], tok_all.at[s], tz_send.at[j], tz_recv.at[j], line_dev(j))
        for j in z_order
    ]

    def tok_set(step, way):
        return tok_all.at[pl.ds(lax.rem(y + ((8 - step) if way == 0 else step), 8) * 4, 4)]

    def tok_on(step, way):
        part = tok_set(step, way)
        remote(part, part, ty_send.at[way, step], ty_recv.at[way, step], y_dev(1 if way == 0 else 7))

    def tok_in(step, way):
        wait_bytes(tok_set(step, way), ty_recv.at[way, step - 1])

    loads[3].wait()
    half_columns = [pl.ds(pl.multiple_of(h * 2048, 2048), 2048) for h in (zh, 1 - zh)]
    proj_half_copy = remote(
        proj_ref.at[:, half_columns[1]], proj_half.at[zh], ph_send.at[0], ph_recv.at[0], half_dev
    )
    proj_half[zh] = proj_ref[:, half_columns[0]]

    loads[2].wait()

    def add_pair(zi, xd):
        own[zi, xd] = (own[zi, xd].astype(F32) + buf_a[zi, xd].astype(F32)).astype(BF16)

    x1, x2, x3 = lax.rem(x + 1, 4), lax.rem(x + 2, 4), lax.rem(x + 3, 4)
    a_copies[0].wait_recv()
    for zi in range(2):
        add_pair(zi, x2)
    b1 = []
    for p, (r0, n) in enumerate(PIECES):
        for zi, k in ((0, 1), (1, 3)):
            b1.append(
                remote(
                    own.at[zi, x2, pl.ds(r0, n)], buf_b1.at[zi, pl.ds(r0, n)],
                    b1_send.at[p, zi], b1_recv.at[p, zi], x_dev(k),
                )
            )
    a_copies[1].wait_recv()
    a_copies[2].wait_recv()
    add_pair(1, x1)
    add_pair(0, x3)
    b2 = {}
    for p, (r0, n) in enumerate(PIECES):
        for zi, xd, k in ((1, x1, 1), (0, x3, 3)):
            b2[p, zi, 0] = remote(
                own.at[zi, xd, pl.ds(r0, n)], buf_b2.at[zi, 0, pl.ds(r0, n)],
                b2_send.at[p, zi, 0], b2_recv.at[p, zi, 0], x_dev(k),
            )
    add_pair(0, x1)
    add_pair(1, x3)

    for copy in tok_z:
        copy.wait_recv()
    for way in range(2):
        tok_on(0, way)
    for p, (r0, n) in enumerate(PIECES):
        for zi, xd, k in ((0, x1, 1), (1, x3, 3)):
            b1[2 * p + zi].wait_recv()
            own[zi, xd, pl.ds(r0, n)] = (
                own[zi, xd, pl.ds(r0, n)].astype(F32) + buf_b1[zi, pl.ds(r0, n)].astype(F32)
            ).astype(BF16)
            b2[p, zi, 1] = remote(
                own.at[zi, xd, pl.ds(r0, n)], buf_b2.at[zi, 1, pl.ds(r0, n)],
                b2_send.at[p, zi, 1], b2_recv.at[p, zi, 1], x_dev(k),
            )
    for way in range(2):
        tok_in(1, way)
        tok_on(1, way)
    a_copies[3].wait_recv()
    for zi in range(2):
        add_pair(zi, x)

    c_copies = []
    for p, (r0, n) in enumerate(PIECES):
        for zi in range(2):
            b2[p, zi, 0].wait_recv()
            b2[p, zi, 1].wait_recv()

        def total_of(zi):
            return (
                own[zi, x, pl.ds(r0, n)].astype(F32)
                + buf_b2[zi, 0, pl.ds(r0, n)].astype(F32)
                + buf_b2[zi, 1, pl.ds(r0, n)].astype(F32)
            )

        send_c[pl.ds(r0, n)] = total_of(1 - zh).astype(BF16)
        c_copies.append(
            remote(
                send_c.at[pl.ds(r0, n)], buf_c.at[pl.ds(r0, n)], c_send.at[p], c_recv.at[p],
                (lax.rem(d + 8, 16), s),
            )
        )
        summed_ref[pl.ds(r0, n)] = total_of(zh)

    proj_half_copy.wait_recv()
    place8 = lax.rem(d, 8)

    def half_block(at):
        return proj_half.at[:, :, pl.ds(pl.multiple_of(at * 256, 256), 256)]

    proj_all[:, place8] = half_block(place8)[...]
    proj_in = few_spread(
        5, proj_all.at[:, pl.ds(0, 7)], lambda i: half_block(lax.rem(dp_peer(i), 8)),
        proj_all.at[:, place8], chip_dev,
    )
    for way in range(2):
        tok_in(2, way)
        tok_on(2, way)
    proj_in()
    loads[4].wait()
    loads[5].wait()
    block = proj_all[...].reshape(256, 256)
    scaled = block.astype(F32) * gain_ref[:, pl.ds(pl.multiple_of(d * 256, 256), 256)]
    high = scaled.astype(BF16)
    low = (scaled - high.astype(F32)).astype(BF16)
    weights = w_ref[...]
    folded = (dot_t(weights, high) + dot_t(weights, low)).astype(BF16)
    gram = dot_t(block, block).astype(BF16)
    for o in range(16):
        if o < 12:
            part_send[o // 8, o % 8, 0:16] = folded[16 * o : 16 * o + 16]
        else:
            part_send[o // 8, o % 8, 0:16] = jnp.zeros((16, 256), BF16)
        part_send[o // 8, o % 8, 16:32] = gram[16 * o : 16 * o + 16]
    part_a[place8] = part_send[:, place8]
    part_in = few_spread(
        0, part_a.at[pl.ds(0, 7)], lambda i: part_send.at[:, lax.rem(dp_peer(i), 8)],
        part_a.at[place8], chip_dev,
    )
    for way in range(2):
        tok_in(3, way)
    tok_on(3, 0)
    squares = jnp.zeros((8, 256), F32)
    for p, (r0, n) in enumerate(PIECES):
        c_copies[p].wait_recv()
        total = summed_ref[pl.ds(r0, n)] + buf_c[pl.ds(r0, n)].astype(F32)
        summed_ref[pl.ds(r0, n)] = total
        squares = squares + jnp.sum((total * total).reshape(n // 8, 8, 256), axis=0)
    tile = squares[:, :128] + squares[:, 128:]
    def share(n, place, tile, device_of):
        sq_mine[n] = tile
        sq_all[n, place] = tile
        arrive = few_spread(
            2 + n, sq_all.at[n, pl.ds(0, 7)], lambda i: sq_mine.at[n], sq_all.at[n, place],
            device_of,
        )

        def total():
            arrive()
            return jnp.sum(sq_all[n], axis=0)

        return total

    sq_sum = share(0, place8, tile, chip_dev)

    part_in()
    half_sum = part_a[0].astype(F32)
    for o in range(1, 8):
        half_sum = half_sum + part_a[o].astype(F32)
    part_sum[...] = half_sum.astype(BF16)
    part_b_copy = remote(part_sum.at[1 - zh], part_b, w_send.at[0], w_recv.at[0], half_dev)

    tok_in(4, 0)
    tokens = tok_all[:, 0, :]
    member = (tokens >> 8) == s
    row_plus = ((tokens & 255) + 1).astype(F32)
    before = (iota((128, 128), 0) < iota((128, 128), 1)).astype(F32).astype(BF16)
    rank = dot(member.astype(F32).astype(BF16), before)
    lane = iota((32, 128), 1)
    want = jnp.zeros((32, 128), F32)
    for k in range(8):
        chosen = jnp.where(member & (rank == float(k)), row_plus, 0.0)
        want = want + jnp.where(lane == k, jnp.sum(chosen, axis=1, keepdims=True), 0.0)
    line = iota((256, 32), 0)
    pick = iota((256, 32), 1) == ((line >> 3) & 1) * 16 + (((line >> 4) - (line & 7)) & 15)
    spread = dot(pick.astype(F32).astype(BF16), want.astype(BF16))
    spread = jnp.where(iota((256, 128), 1) == (iota((256, 128), 0) & 7), spread, 0.0)
    idx_send[...] = dot(spread.astype(BF16), jnp.ones((128, 128), BF16)).astype(BF16)
    mine16 = pl.ds(pl.multiple_of(d * 16, 16), 16)
    idx_all[mine16] = idx_send[mine16]
    idx_in = dp_spread(
        0,
        idx_all.at[pl.ds(0, 240)],
        lambda peer: idx_send.at[pl.ds(pl.multiple_of(peer * 16, 16), 16)],
        idx_all.at[mine16],
    )

    owner_row = (tok >> 8).astype(F32)
    owner_line = jnp.broadcast_to(owner_row, (128, 128))
    owner_col = owner_line.T
    earlier = iota((128, 128), 1) < iota((128, 128), 0)
    slot = jnp.sum(jnp.where((owner_col == owner_line) & earlier, 1.0, 0.0), axis=1, keepdims=True)
    place = owner_col[:, 0:1] * 16.0 + slot
    at = iota((128, 512), 1).astype(F32)
    find_left = jnp.where(at == place, 1.0, 0.0).astype(BF16)
    find_right = jnp.where(at == place + 8.0, 1.0, 0.0).astype(BF16)

    sq_sum = share(1, zh * 4 + z, sq_sum(), far_dev)

    line, col = iota((512, 256), 0), iota((512, 256), 1)
    to, unit = line >> 4, line & 15
    k = unit & 7
    match = col == ((to + k) & 15) * 16 + (to >> 4) * 8 + k
    pack_left = jnp.where(match & (unit < 8), 1.0, 0.0).astype(BF16)
    pack_right = jnp.where(match & (unit >= 8), 1.0, 0.0).astype(BF16)
    part_b_copy.wait_recv()
    w_pair[zh] = (part_sum[zh].astype(F32) + part_b[...].astype(F32)).astype(BF16)
    w_pair_copy = remote(w_pair.at[zh], w_pair.at[zh], w_send.at[1], w_recv.at[1], half_dev)

    sq_sum = share(2, y, sq_sum(), y_dev)
    idx_in()
    ids = idx_all[...].astype(F32)
    for half in range(2):
        at = (iota((256, 128), 1) + 1 + 128 * half).astype(F32)
        onehot[:, 128 * half : 128 * half + 128] = jnp.where(ids == at, 1.0, 0.0).astype(BF16)

    for load in loads[6:]:
        load.wait()

    total = sq_sum()
    total = jnp.sum(jnp.sum(total, axis=0, keepdims=True), axis=1, keepdims=True)
    clip = jnp.minimum(1.0, 0.2 * math.sqrt(TOTAL_ENTRIES) / (jnp.sqrt(total) + 1e-06))
    grad = clip * summed_ref[...]
    new_m1 = 0.9 * state[1] + 0.1 * grad
    new_m2 = 0.95 * state[2] + 0.05 * grad * grad
    one = new_m1 * (1.0 / (1.0 - 0.9**10))
    two = new_m2 * (1.0 / (1.0 - 0.95**10))
    master = state[0]
    new_master = master - 0.01 * (one / (jnp.sqrt(two) + 1e-08) + 0.1 * master)
    table = new_master.astype(BF16)
    found = dot(onehot[:, 0:ROWS], table).astype(BF16)
    rows_send[...] = found
    rows_in = dp_spread(
        1,
        rows_all.at[pl.ds(0, 240)],
        lambda peer: rows_send.at[pl.ds(pl.multiple_of(peer * 16, 16), 16)],
        rows_all.at[mine16],
    )
    rows_all[mine16] = rows_send[mine16]
    w_pair_copy.wait_recv()
    w_all[:, place8] = w_pair[...]
    weights_in = few_spread(
        1, w_all.at[:, pl.ds(0, 7)], lambda i: w_pair, w_all.at[:, place8], chip_dev
    )
    state[0] = new_master
    state[1] = new_m1
    state[2] = new_m2
    for n, ref in enumerate((o_master, o_m1, o_m2)):
        store = pltpu.make_async_copy(state.at[n], ref, out_sem.at[n])
        store.start()
        sent.append(store.wait)
    settle(len(sent) - 5)
    rows_in()
    rows = rows_all[...]
    back_send[...] = (dot(pack_left, rows[:, :128]) + dot(pack_right, rows[:, 128:])).astype(BF16)
    mine_s = pl.ds(pl.multiple_of(s * 16, 16), 16)
    back_in = sh_spread(
        0,
        back_all.at[pl.ds(0, 496)],
        lambda peer: back_send.at[pl.ds(pl.multiple_of(peer * 16, 16), 16)],
        back_all.at[mine_s],
    )
    back_all[mine_s] = back_send[mine_s]
    settle(len(sent) - 1)
    weights_in()
    gram = w_all[:, :, 16:32, :].reshape(256, 256)
    folded = w_all[:, :, 0:16, :].reshape(256, 256)[0:192]
    back_in()
    back = back_all[...]
    rows = jnp.concatenate([dot(find_left, back), dot(find_right, back)], axis=1)
    mean_sq = jnp.sum(dot(rows.astype(BF16), gram) * rows, axis=1, keepdims=True) / 4096.0
    gathered[s] = (rows * lax.rsqrt(mean_sq + 1e-05)).astype(BF16)

    first, last = pl.ds(0, FIRST), pl.ds(FIRST, 128 - FIRST)

    def block_at(step, way, j):
        back_by = (8 - step) if way == 0 else step
        return lax.rem(y + back_by, 8) * 4 + z_of(j)

    def ring_to(way):
        return y_dev(1 if way == 0 else 7)

    def first_on(step, way, j):
        part = gathered.at[block_at(step, way, j), first]
        remote(part, part, y_send.at[way, step, j], y_recv.at[way, step, j], ring_to(way))

    def first_in(step, way, j):
        part = gathered.at[block_at(step, way, j), first]
        wait_bytes(part, y_recv.at[way, step - 1, j])

    def last_rows(step, way):
        if step < 3:
            return last
        return pl.ds(FIRST + way * 32, 32 - 16 * way)

    def last_on(step, way):
        part = gathered.at[block_at(step, way, 0), last_rows(step, way)]
        remote(part, part, yl_send.at[way, step], yl_recv.at[way, step], ring_to(way))

    def last_in(step, way):
        part = gathered.at[block_at(step, way, 0), last_rows(step - 1, way)]
        wait_bytes(part, yl_recv.at[way, step - 1])

    def last_along_z(step, way):
        part = gathered.at[block_at(step, way, 0), last]
        for j in z_order:
            remote(
                part, part, zl_send.at[way, step - 1, j], zl_recv.at[way, step - 1, j],
                (d, y * 4 + z_of(j)),
            )

    def project(step, way, j):
        at = block_at(step, way, j)
        if step and j:
            wait_bytes(gathered.at[at, last], zl_recv.at[way, step - 1, j])
        columns = pl.ds(pl.multiple_of(at * 128, 128), 128)
        qkv[:, columns] = dot_t(folded, gathered[at]).astype(BF16)
        pltpu.make_async_copy(qkv.at[:, columns], o_q.at[:, columns], out_sem.at[3]).start()

    def own_along_z(rows, n):
        part = gathered.at[s, rows]
        for j in z_order:
            remote(part, part, z_send.at[n, j], z_recv.at[n, j], (d, y * 4 + z_of(j)))

    own_along_z(first, 0)
    for way in range(2):
        first_on(0, way, 0)
    for way in range(2):
        last_on(0, way)
    own_along_z(last, 1)
    project(0, 0, 0)
    for j in z_order:
        wait_bytes(gathered.at[block_at(0, 0, j), first], z_recv.at[0, j])
        for way in range(2):
            first_on(0, way, j)
    for j in z_order:
        wait_bytes(gathered.at[block_at(0, 0, j), last], z_recv.at[1, j])
    marks = [len(sent)]
    for step in (1, 2, 3):
        for way in range(2):
            last_in(step, way)
            last_on(step, way)
            last_along_z(step, way)
        for j in (0,) + z_order:
            for way in range(2):
                first_in(step, way, j)
                if step < 3 or j // 2 == way:
                    first_on(step, way, j)
        if step == 1:
            for j in z_order:
                project(0, 0, j)
        else:
            for j in range(4):
                for way in range(2):
                    project(step - 1, way, j)
        if step == 3:
            settle(marks[1])
        marks.append(len(sent))
    for way in range(2):
        last_in(4, way)
    last_along_z(4, 0)
    for j in range(4):
        for way in range(2):
            project(3, way, j)
    for j in (0, 3, 1, 2):
        first_in(4, j // 2, j)
        project(4, 0, j)

    wait_bytes(qkv, out_sem.at[3])
    for wait in sent:
        wait()


def store_kernel(*refs):
    sources, targets, held, sem = refs[:4], refs[4:8], refs[8:12], refs[12]
    parts = [(n, slice(None)) for n in range(3)] + [(3, pl.ds(1024 * c, 1024)) for c in range(4)]
    loads = [
        pltpu.make_async_copy(sources[n].at[:, at], held[n].at[:, at], sem.at[0, i])
        for i, (n, at) in enumerate(parts)
    ]
    stores = [
        pltpu.make_async_copy(held[n].at[:, at], targets[n].at[:, at], sem.at[1, i])
        for i, (n, at) in enumerate(parts)
    ]
    for load in loads:
        load.start()
    for load, store in zip(loads, stores):
        load.wait()
        store.start()
    for store in stores:
        store.wait()


def body(grad_groups, master, moment1, moment2, proj, ln_gain, w_qkv, token_owner, token_row):
    hbm = pl.BlockSpec(memory_space=pltpu.HBM)
    dma = pltpu.SemaphoreType.DMA
    results = pl.pallas_call(
        kernel,
        out_shape=(
            jax.ShapeDtypeStruct((ROWS, 256), F32),
            jax.ShapeDtypeStruct((ROWS, 256), F32),
            jax.ShapeDtypeStruct((ROWS, 256), F32),
            jax.ShapeDtypeStruct((192, 4096), BF16),
        ),
        in_specs=[hbm] * 9,
        out_specs=[hbm] * 4,
        scratch_shapes=[
            pltpu.VMEM((16, 4096), BF16),
            pltpu.VMEM((1, 4096), F32),
            pltpu.VMEM((192, 256), BF16),
            pltpu.VMEM((1, 128), jnp.int32),
            pltpu.VMEM((1, 128), jnp.int32),
            pltpu.VMEM((2, 4, ROWS, 256), BF16),
            pltpu.VMEM((2, 4, ROWS, 256), BF16),
            pltpu.VMEM((2, ROWS, 256), BF16),
            pltpu.VMEM((2, 2, ROWS, 256), BF16),
            pltpu.VMEM((ROWS, 256), BF16),
            pltpu.VMEM((ROWS, 256), BF16),
            pltpu.VMEM((3, ROWS, 256), F32),
            pltpu.VMEM((ROWS, 256), F32),
            pltpu.VMEM((32, 8, 128), jnp.int32),
            pltpu.VMEM((256, 128), BF16),
            pltpu.VMEM((256, 128), BF16),
            pltpu.VMEM((256, 256), BF16),
            pltpu.VMEM((2, 16, 2048), BF16),
            pltpu.VMEM((2, 8, 16, 256), BF16),
            pltpu.VMEM((2, 8, 32, 256), BF16),
            pltpu.VMEM((8, 2, 32, 256), BF16),
            pltpu.VMEM((2, 32, 256), BF16),
            pltpu.VMEM((32, 256), BF16),
            pltpu.VMEM((2, 32, 256), BF16),
            pltpu.VMEM((2, 8, 32, 256), BF16),
            pltpu.VMEM((3, 8, 128), F32),
            pltpu.VMEM((3, 8, 8, 128), F32),
            pltpu.VMEM((256, 256), BF16),
            pltpu.VMEM((256, 256), BF16),
            pltpu.VMEM((512, 128), BF16),
            pltpu.VMEM((512, 128), BF16),
            pltpu.VMEM((32, 128, 256), BF16),
            pltpu.VMEM((192, 4096), BF16),
            dma((9,)),
            dma((4,)),
            dma((4,)), dma((4,)),
            dma((len(PIECES), 2)), dma((len(PIECES), 2)),
            dma((len(PIECES), 2, 2)), dma((len(PIECES), 2, 2)),
            dma((len(PIECES),)), dma((len(PIECES),)),
            dma((2,)), dma((2,)),
            dma((1,)), dma((1,)),
            dma((6,)), dma((6,)),
            dma((2,)), dma((2,)),
            dma((4,)), dma((4,)),
            dma((2, 4)), dma((2, 4)),
            dma((1,)), dma((1,)),
            dma((2, 4)), dma((2, 4)),
            dma((2, 4, 4)), dma((2, 4, 4)),
            dma((2, 4)), dma((2, 4)),
            dma((2, 4, 4)), dma((2, 4, 4)),
        ],
        compiler_params=pltpu.CompilerParams(
            collective_id=0, has_side_effects=True, vmem_limit_bytes=56 << 20
        ),
        name="step",
    )(
        grad_groups.reshape(2, 4, 2, ROWS, 256),
        master,
        moment1,
        moment2,
        proj,
        ln_gain.reshape(1, 4096),
        w_qkv.T,
        token_owner.reshape(1, 128),
        token_row.reshape(1, 128),
    )
    new_master, new_m1, new_m2, qkv_t = pl.pallas_call(
        store_kernel,
        out_shape=tuple(jax.ShapeDtypeStruct(a.shape, a.dtype) for a in results),
        in_specs=[pl.BlockSpec(memory_space=pl.ANY)] * 4,
        out_specs=[hbm] * 4,
        scratch_shapes=[pltpu.VMEM(a.shape, a.dtype) for a in results] + [dma((2, 7))],
        name="store",
    )(*results)
    return new_master, new_m1, new_m2, qkv_t.T


def solution(mesh):
    placed = (
        P("dp", "shard", None),
        P(("shard", "dp"), None),
        P(("shard", "dp"), None),
        P(("shard", "dp"), None),
        P("dp", None),
        P(),
        P("dp", "shard"),
        P(("dp", "shard"), None),
        P(("dp", "shard")),
    )
    return jax.shard_map(
        body,
        mesh=mesh,
        in_specs=placed,
        out_specs=(
            P(("shard", "dp"), None),
            P(("shard", "dp"), None),
            P(("shard", "dp"), None),
            P("dp", "shard"),
        ),
        check_vma=False,
    )
```

```python
import math

import jax
import jax.numpy as jnp
from jax import lax
from jax.experimental import pallas as pl
from jax.experimental.pallas import tpu as pltpu
from jax.sharding import PartitionSpec as P

MESH = pl.DeviceIdType.MESH
F32 = jnp.float32
BF16 = jnp.bfloat16
ROWS = 208
FIRST = 80
FAR_FIRST = sorted(range(1, 32), key=lambda i: -min(i // 4, 8 - i // 4) - (i % 4 > 0))
PIECES = ((0, 128), (128, 80))
TOTAL_ENTRIES = 106496 * 256


def dot(a, b):
    return lax.dot_general(a, b, (((1,), (0,)), ((), ())), preferred_element_type=F32)


def dot_t(a, b):
    return lax.dot_general(a, b, (((1,), (1,)), ((), ())), preferred_element_type=F32)


def iota(shape, axis):
    return lax.broadcasted_iota(jnp.int32, shape, axis)


def kernel(
    g_ref, master_ref, m1_ref, m2_ref, proj_hbm, gain_hbm, w_hbm, owner_hbm, row_hbm,
    o_master, o_m1, o_m2, o_q,
    proj_ref, gain_ref, w_ref, owner_ref, row_ref,
    own, buf_a, buf_b1, buf_b2, send_c, buf_c, state, summed_ref,
    tok_all, idx_send, idx_all, onehot, proj_half, proj_all, part_send, part_a, part_sum, part_b, w_pair, w_all,
    sq_mine, sq_all, rows_send, rows_all, back_send, back_all, gathered, qkv,
    local_sem, out_sem, a_send, a_recv, b1_send, b1_recv, b2_send, b2_recv, c_send, c_recv,
    dp_send, dp_recv, sh_send, sh_recv, few_send, few_recv, w_send, w_recv,
    tz_send, tz_recv, ty_send, ty_recv, ph_send, ph_recv, z_send, z_recv, y_send, y_recv, yl_send, yl_recv, zl_send, zl_recv,
):
    d = lax.axis_index("dp")
    s = lax.axis_index("shard")
    core, x, zh = lax.rem(d, 2), lax.rem(d // 2, 4), d // 8
    y, z = s // 4, lax.rem(s, 4)

    def dp_peer(i):
        kz, kx, kc = i // 8, lax.rem(i // 2, 4), lax.rem(i, 2)
        return lax.rem(zh + kz, 2) * 8 + lax.rem(x + kx, 4) * 2 + lax.rem(core + kc, 2)

    def sh_peer(i):
        return lax.rem(y + i // 4, 8) * 4 + lax.rem(z + lax.rem(i, 4), 4)

    def far_dev(i):
        at = lax.rem(zh * 4 + z + i, 8)
        return ((at // 4) * 8 + lax.rem(d, 8), y * 4 + lax.rem(at, 4))

    def x_dev(k):
        return (zh * 8 + lax.rem(x + k, 4) * 2 + core, s)

    def y_dev(k):
        return (d, lax.rem(y + k, 8) * 4 + z)

    loads = []
    for n, (src, dst) in enumerate(
        (
            (owner_hbm, owner_ref), (row_hbm, row_ref), (g_ref.at[:, :, core], own),
            (proj_hbm, proj_ref), (w_hbm, w_ref), (gain_hbm, gain_ref),
            (master_ref, state.at[0]), (m1_ref, state.at[1]), (m2_ref, state.at[2]),
        )
    ):
        load = pltpu.make_async_copy(src, dst, local_sem.at[n])
        load.start()
        loads.append(load)

    def z_of(j):
        return (z, z + 1 - 2 * lax.rem(z, 2), lax.rem(z + 2, 4), 3 - z)[j]

    z_order = (1, 3, 2)
    half_dev = (lax.rem(d + 8, 16), s)

    def line_dev(j):
        return (d, y * 4 + z_of(j))

    barrier = pltpu.get_barrier_semaphore()
    first_devs = [(d + 1 - 2 * core, s), x_dev(1), x_dev(3), half_dev, y_dev(1), y_dev(7)]
    first_devs += [line_dev(j) for j in z_order]
    for dev in first_devs:
        pl.semaphore_signal(barrier, inc=1, device_id=dev, device_id_type=MESH)
    pl.semaphore_wait(barrier, len(first_devs))

    sent = []

    def settle(count):
        for wait in sent[:count]:
            wait()
        del sent[:count]


    def copy_to(src, dst, send_sem, recv_sem, device):
        return pltpu.make_async_remote_copy(
            src_ref=src, dst_ref=dst, send_sem=send_sem, recv_sem=recv_sem,
            device_id=device, device_id_type=MESH,
        )

    def remote(src, dst, send_sem, recv_sem, device):
        copy = copy_to(src, dst, send_sem, recv_sem, device)
        copy.start()
        sent.append(copy.wait_send)
        return copy

    def dp_spread(phase, batch, src_of, dst):
        for i in range(15, 0, -1):
            peer = dp_peer(i)
            copy_to(src_of(peer), dst, dp_send.at[phase], dp_recv.at[phase], (peer, s)).start()
        sent.append(lambda: wait_bytes(batch, dp_send.at[phase]))
        return lambda: wait_bytes(batch, dp_recv.at[phase])

    def sh_spread(phase, batch, src_of, dst):
        for i in FAR_FIRST:
            peer = sh_peer(i)
            copy_to(src_of(peer), dst, sh_send.at[phase], sh_recv.at[phase], (d, peer)).start()
        sent.append(lambda: wait_bytes(batch, sh_send.at[phase]))
        return lambda: wait_bytes(batch, sh_recv.at[phase])

    def few_spread(phase, batch, src_of, dst, device_of):
        for i in range(7, 0, -1):
            copy_to(src_of(i), dst, few_send.at[phase], few_recv.at[phase], device_of(i)).start()
        sent.append(lambda: wait_bytes(batch, few_send.at[phase]))
        return lambda: wait_bytes(batch, few_recv.at[phase])

    def chip_dev(i):
        return (dp_peer(i), s)

    def wait_bytes(ref, sem):
        pltpu.make_async_copy(ref, ref, sem).wait()

    a_copies = []
    for n, k in enumerate((2, 1, 3, 0)):
        xd = lax.rem(x + k, 4)
        a_copies.append(
            remote(
                g_ref.at[:, xd, 1 - core], buf_a.at[:, xd], a_send.at[n], a_recv.at[n],
                (d + 1 - 2 * core, s),
            )
        )

    loads[0].wait()
    loads[1].wait()
    tok = owner_ref[...] * 256 + row_ref[...]
    tok_all[s] = jnp.broadcast_to(tok, (8, 128))
    tok_z = [
        remote(tok_all.at[s], tok_all.at[s], tz_send.at[j], tz_recv.at[j], line_dev(j))
        for j in z_order
    ]

    def tok_set(step, way):
        return tok_all.at[pl.ds(lax.rem(y + ((8 - step) if way == 0 else step), 8) * 4, 4)]

    def tok_on(step, way):
        part = tok_set(step, way)
        remote(part, part, ty_send.at[way, step], ty_recv.at[way, step], y_dev(1 if way == 0 else 7))

    def tok_in(step, way):
        wait_bytes(tok_set(step, way), ty_recv.at[way, step - 1])

    loads[3].wait()
    half_columns = [pl.ds(pl.multiple_of(h * 2048, 2048), 2048) for h in (zh, 1 - zh)]
    proj_half_copy = remote(
        proj_ref.at[:, half_columns[1]], proj_half.at[zh], ph_send.at[0], ph_recv.at[0], half_dev
    )
    proj_half[zh] = proj_ref[:, half_columns[0]]

    loads[2].wait()

    def add_pair(zi, xd):
        own[zi, xd] = (own[zi, xd].astype(F32) + buf_a[zi, xd].astype(F32)).astype(BF16)

    x1, x2, x3 = lax.rem(x + 1, 4), lax.rem(x + 2, 4), lax.rem(x + 3, 4)
    a_copies[0].wait_recv()
    for zi in range(2):
        add_pair(zi, x2)
    b1 = []
    for p, (r0, n) in enumerate(PIECES):
        for zi, k in ((0, 1), (1, 3)):
            b1.append(
                remote(
                    own.at[zi, x2, pl.ds(r0, n)], buf_b1.at[zi, pl.ds(r0, n)],
                    b1_send.at[p, zi], b1_recv.at[p, zi], x_dev(k),
                )
            )
    a_copies[1].wait_recv()
    a_copies[2].wait_recv()
    add_pair(1, x1)
    add_pair(0, x3)
    b2 = {}
    for p, (r0, n) in enumerate(PIECES):
        for zi, xd, k in ((1, x1, 1), (0, x3, 3)):
            b2[p, zi, 0] = remote(
                own.at[zi, xd, pl.ds(r0, n)], buf_b2.at[zi, 0, pl.ds(r0, n)],
                b2_send.at[p, zi, 0], b2_recv.at[p, zi, 0], x_dev(k),
            )
    add_pair(0, x1)
    add_pair(1, x3)

    for copy in tok_z:
        copy.wait_recv()
    for way in range(2):
        tok_on(0, way)
    for p, (r0, n) in enumerate(PIECES):
        for zi, xd, k in ((0, x1, 1), (1, x3, 3)):
            b1[2 * p + zi].wait_recv()
            own[zi, xd, pl.ds(r0, n)] = (
                own[zi, xd, pl.ds(r0, n)].astype(F32) + buf_b1[zi, pl.ds(r0, n)].astype(F32)
            ).astype(BF16)
            b2[p, zi, 1] = remote(
                own.at[zi, xd, pl.ds(r0, n)], buf_b2.at[zi, 1, pl.ds(r0, n)],
                b2_send.at[p, zi, 1], b2_recv.at[p, zi, 1], x_dev(k),
            )
    for way in range(2):
        tok_in(1, way)
        tok_on(1, way)
    a_copies[3].wait_recv()
    for zi in range(2):
        add_pair(zi, x)

    c_copies = []
    for p, (r0, n) in enumerate(PIECES):
        for zi in range(2):
            b2[p, zi, 0].wait_recv()
            b2[p, zi, 1].wait_recv()

        def total_of(zi):
            return (
                own[zi, x, pl.ds(r0, n)].astype(F32)
                + buf_b2[zi, 0, pl.ds(r0, n)].astype(F32)
                + buf_b2[zi, 1, pl.ds(r0, n)].astype(F32)
            )

        send_c[pl.ds(r0, n)] = total_of(1 - zh).astype(BF16)
        c_copies.append(
            remote(
                send_c.at[pl.ds(r0, n)], buf_c.at[pl.ds(r0, n)], c_send.at[p], c_recv.at[p],
                (lax.rem(d + 8, 16), s),
            )
        )
        summed_ref[pl.ds(r0, n)] = total_of(zh)

    proj_half_copy.wait_recv()
    place8 = lax.rem(d, 8)

    def half_block(at):
        return proj_half.at[:, :, pl.ds(pl.multiple_of(at * 256, 256), 256)]

    proj_all[:, place8] = half_block(place8)[...]
    proj_in = few_spread(
        5, proj_all.at[:, pl.ds(0, 7)], lambda i: half_block(lax.rem(dp_peer(i), 8)),
        proj_all.at[:, place8], chip_dev,
    )
    for way in range(2):
        tok_in(2, way)
        tok_on(2, way)
    proj_in()
    loads[4].wait()
    loads[5].wait()
    block = proj_all[...].reshape(256, 256)
    scaled = block.astype(F32) * gain_ref[:, pl.ds(pl.multiple_of(d * 256, 256), 256)]
    high = scaled.astype(BF16)
    low = (scaled - high.astype(F32)).astype(BF16)
    weights = w_ref[...]
    folded = (dot_t(weights, high) + dot_t(weights, low)).astype(BF16)
    gram = dot_t(block, block).astype(BF16)
    for o in range(16):
        if o < 12:
            part_send[o // 8, o % 8, 0:16] = folded[16 * o : 16 * o + 16]
        else:
            part_send[o // 8, o % 8, 0:16] = jnp.zeros((16, 256), BF16)
        part_send[o // 8, o % 8, 16:32] = gram[16 * o : 16 * o + 16]
    part_a[place8] = part_send[:, place8]
    part_in = few_spread(
        0, part_a.at[pl.ds(0, 7)], lambda i: part_send.at[:, lax.rem(dp_peer(i), 8)],
        part_a.at[place8], chip_dev,
    )
    for way in range(2):
        tok_in(3, way)
    tok_on(3, 0)
    squares = jnp.zeros((8, 256), F32)
    for p, (r0, n) in enumerate(PIECES):
        c_copies[p].wait_recv()
        total = summed_ref[pl.ds(r0, n)] + buf_c[pl.ds(r0, n)].astype(F32)
        summed_ref[pl.ds(r0, n)] = total
        squares = squares + jnp.sum((total * total).reshape(n // 8, 8, 256), axis=0)
    tile = jnp.sum(squares[:, :128] + squares[:, 128:], axis=0, keepdims=True)
    def share(n, place, tile, device_of):
        sq_mine[n] = tile
        sq_all[n, place] = tile
        arrive = few_spread(
            2 + n, sq_all.at[n, pl.ds(0, 7)], lambda i: sq_mine.at[n], sq_all.at[n, place],
            device_of,
        )

        def total():
            arrive()
            return jnp.sum(sq_all[n], axis=0)

        return total

    sq_sum = share(0, place8, tile, chip_dev)

    part_in()
    half_sum = part_a[0].astype(F32)
    for o in range(1, 8):
        half_sum = half_sum + part_a[o].astype(F32)
    part_sum[...] = half_sum.astype(BF16)
    part_b_copy = remote(part_sum.at[1 - zh], part_b, w_send.at[0], w_recv.at[0], half_dev)

    tok_in(4, 0)
    tokens = tok_all[:, 0, :]
    member = (tokens >> 8) == s
    row_plus = ((tokens & 255) + 1).astype(F32)
    before = (iota((128, 128), 0) < iota((128, 128), 1)).astype(F32).astype(BF16)
    rank = dot(member.astype(F32).astype(BF16), before)
    lane = iota((32, 128), 1)
    want = jnp.zeros((32, 128), F32)
    for k in range(8):
        chosen = jnp.where(member & (rank == float(k)), row_plus, 0.0)
        want = want + jnp.where(lane == k, jnp.sum(chosen, axis=1, keepdims=True), 0.0)
    line = iota((256, 32), 0)
    pick = iota((256, 32), 1) == ((line >> 3) & 1) * 16 + (((line >> 4) - (line & 7)) & 15)
    spread = dot(pick.astype(F32).astype(BF16), want.astype(BF16))
    spread = jnp.where(iota((256, 128), 1) == (iota((256, 128), 0) & 7), spread, 0.0)
    idx_send[...] = dot(spread.astype(BF16), jnp.ones((128, 128), BF16)).astype(BF16)
    mine16 = pl.ds(pl.multiple_of(d * 16, 16), 16)
    idx_all[mine16] = idx_send[mine16]
    idx_in = dp_spread(
        0,
        idx_all.at[pl.ds(0, 240)],
        lambda peer: idx_send.at[pl.ds(pl.multiple_of(peer * 16, 16), 16)],
        idx_all.at[mine16],
    )

    owner_row = (tok >> 8).astype(F32)
    owner_line = jnp.broadcast_to(owner_row, (128, 128))
    owner_col = owner_line.T
    earlier = iota((128, 128), 1) < iota((128, 128), 0)
    slot = jnp.sum(jnp.where((owner_col == owner_line) & earlier, 1.0, 0.0), axis=1, keepdims=True)
    place = owner_col[:, 0:1] * 16.0 + slot
    at = iota((128, 512), 1).astype(F32)
    find_left = jnp.where(at == place, 1.0, 0.0).astype(BF16)
    find_right = jnp.where(at == place + 8.0, 1.0, 0.0).astype(BF16)

    sq_sum = share(1, zh * 4 + z, sq_sum(), far_dev)

    line, col = iota((512, 256), 0), iota((512, 256), 1)
    to, unit = line >> 4, line & 15
    k = unit & 7
    match = col == ((to + k) & 15) * 16 + (to >> 4) * 8 + k
    pack_left = jnp.where(match & (unit < 8), 1.0, 0.0).astype(BF16)
    pack_right = jnp.where(match & (unit >= 8), 1.0, 0.0).astype(BF16)
    part_b_copy.wait_recv()
    w_pair[zh] = (part_sum[zh].astype(F32) + part_b[...].astype(F32)).astype(BF16)
    w_pair_copy = remote(w_pair.at[zh], w_pair.at[zh], w_send.at[1], w_recv.at[1], half_dev)

    sq_sum = share(2, y, sq_sum(), y_dev)
    idx_in()
    ids = idx_all[...].astype(F32)
    for half in range(2):
        at = (iota((256, 128), 1) + 1 + 128 * half).astype(F32)
        onehot[:, 128 * half : 128 * half + 128] = jnp.where(ids == at, 1.0, 0.0).astype(BF16)

    for load in loads[6:]:
        load.wait()

    total = sq_sum()
    total = jnp.sum(jnp.sum(total, axis=0, keepdims=True), axis=1, keepdims=True)
    clip = jnp.minimum(1.0, 0.2 * math.sqrt(TOTAL_ENTRIES) / (jnp.sqrt(total) + 1e-06))
    grad = clip * summed_ref[...]
    new_m1 = 0.9 * state[1] + 0.1 * grad
    new_m2 = 0.95 * state[2] + 0.05 * grad * grad
    one = new_m1 * (1.0 / (1.0 - 0.9**10))
    two = new_m2 * (1.0 / (1.0 - 0.95**10))
    master = state[0]
    new_master = master - 0.01 * (one / (jnp.sqrt(two) + 1e-08) + 0.1 * master)
    table = new_master.astype(BF16)
    found = dot(onehot[:, 0:ROWS], table).astype(BF16)
    rows_send[...] = found
    rows_in = dp_spread(
        1,
        rows_all.at[pl.ds(0, 240)],
        lambda peer: rows_send.at[pl.ds(pl.multiple_of(peer * 16, 16), 16)],
        rows_all.at[mine16],
    )
    rows_all[mine16] = rows_send[mine16]
    w_pair_copy.wait_recv()
    w_all[:, place8] = w_pair[...]
    weights_in = few_spread(
        1, w_all.at[:, pl.ds(0, 7)], lambda i: w_pair, w_all.at[:, place8], chip_dev
    )
    state[0] = new_master
    state[1] = new_m1
    state[2] = new_m2
    for n, ref in enumerate((o_master, o_m1, o_m2)):
        store = pltpu.make_async_copy(state.at[n], ref, out_sem.at[n])
        store.start()
        sent.append(store.wait)
    settle(len(sent) - 5)
    rows_in()
    rows = rows_all[...]
    back_send[...] = (dot(pack_left, rows[:, :128]) + dot(pack_right, rows[:, 128:])).astype(BF16)
    mine_s = pl.ds(pl.multiple_of(s * 16, 16), 16)
    back_in = sh_spread(
        0,
        back_all.at[pl.ds(0, 496)],
        lambda peer: back_send.at[pl.ds(pl.multiple_of(peer * 16, 16), 16)],
        back_all.at[mine_s],
    )
    back_all[mine_s] = back_send[mine_s]
    settle(len(sent) - 1)
    weights_in()
    gram = w_all[:, :, 16:32, :].reshape(256, 256)
    folded = w_all[:, :, 0:16, :].reshape(256, 256)[0:192]
    back_in()
    back = back_all[...]
    rows = jnp.concatenate([dot(find_left, back), dot(find_right, back)], axis=1)
    mean_sq = jnp.sum(dot(rows.astype(BF16), gram) * rows, axis=1, keepdims=True) / 4096.0
    gathered[s] = (rows * lax.rsqrt(mean_sq + 1e-05)).astype(BF16)

    first, last = pl.ds(0, FIRST), pl.ds(FIRST, 128 - FIRST)

    def block_at(step, way, j):
        back_by = (8 - step) if way == 0 else step
        return lax.rem(y + back_by, 8) * 4 + z_of(j)

    def ring_to(way):
        return y_dev(1 if way == 0 else 7)

    def first_on(step, way, j):
        part = gathered.at[block_at(step, way, j), first]
        remote(part, part, y_send.at[way, step, j], y_recv.at[way, step, j], ring_to(way))

    def first_in(step, way, j):
        part = gathered.at[block_at(step, way, j), first]
        wait_bytes(part, y_recv.at[way, step - 1, j])

    def last_rows(step, way):
        if step < 3:
            return last
        return pl.ds(FIRST + way * 32, 32 - 16 * way)

    def last_on(step, way):
        part = gathered.at[block_at(step, way, 0), last_rows(step, way)]
        remote(part, part, yl_send.at[way, step], yl_recv.at[way, step], ring_to(way))

    def last_in(step, way):
        part = gathered.at[block_at(step, way, 0), last_rows(step - 1, way)]
        wait_bytes(part, yl_recv.at[way, step - 1])

    def last_along_z(step, way):
        part = gathered.at[block_at(step, way, 0), last]
        for j in z_order:
            remote(
                part, part, zl_send.at[way, step - 1, j], zl_recv.at[way, step - 1, j],
                (d, y * 4 + z_of(j)),
            )

    def project(step, way, j):
        at = block_at(step, way, j)
        if step and j:
            wait_bytes(gathered.at[at, last], zl_recv.at[way, step - 1, j])
        columns = pl.ds(pl.multiple_of(at * 128, 128), 128)
        qkv[:, columns] = dot_t(folded, gathered[at]).astype(BF16)
        pltpu.make_async_copy(qkv.at[:, columns], o_q.at[:, columns], out_sem.at[3]).start()

    def own_along_z(rows, n):
        part = gathered.at[s, rows]
        for j in z_order:
            remote(part, part, z_send.at[n, j], z_recv.at[n, j], (d, y * 4 + z_of(j)))

    own_along_z(first, 0)
    for way in range(2):
        first_on(0, way, 0)
    for way in range(2):
        last_on(0, way)
    own_along_z(last, 1)
    project(0, 0, 0)
    for j in z_order:
        wait_bytes(gathered.at[block_at(0, 0, j), first], z_recv.at[0, j])
        for way in range(2):
            first_on(0, way, j)
    for j in z_order:
        wait_bytes(gathered.at[block_at(0, 0, j), last], z_recv.at[1, j])
    marks = [len(sent)]
    for step in (1, 2, 3):
        for way in range(2):
            last_in(step, way)
            last_on(step, way)
            last_along_z(step, way)
        for j in (0,) + z_order:
            for way in range(2):
                first_in(step, way, j)
                if step < 3 or j // 2 == way:
                    first_on(step, way, j)
        if step == 1:
            for j in z_order:
                project(0, 0, j)
        else:
            for j in range(4):
                for way in range(2):
                    project(step - 1, way, j)
        if step == 3:
            settle(marks[1])
        marks.append(len(sent))
    for way in range(2):
        last_in(4, way)
    last_along_z(4, 0)
    for j in range(4):
        for way in range(2):
            project(3, way, j)
    for j in (0, 3, 1, 2):
        first_in(4, j // 2, j)
        project(4, 0, j)

    wait_bytes(qkv, out_sem.at[3])
    for wait in sent:
        wait()


def store_kernel(*refs):
    sources, targets, held, sem = refs[:4], refs[4:8], refs[8:12], refs[12]
    parts = [(n, slice(None)) for n in range(3)] + [(3, pl.ds(2048 * c, 2048)) for c in range(2)]
    loads = [
        pltpu.make_async_copy(sources[n].at[:, at], held[n].at[:, at], sem.at[0, i])
        for i, (n, at) in enumerate(parts)
    ]
    stores = [
        pltpu.make_async_copy(held[n].at[:, at], targets[n].at[:, at], sem.at[1, i])
        for i, (n, at) in enumerate(parts)
    ]
    for load in loads:
        load.start()
    for load, store in zip(loads, stores):
        load.wait()
        store.start()
    for store in stores:
        store.wait()


def body(grad_groups, master, moment1, moment2, proj, ln_gain, w_qkv, token_owner, token_row):
    hbm = pl.BlockSpec(memory_space=pltpu.HBM)
    dma = pltpu.SemaphoreType.DMA
    results = pl.pallas_call(
        kernel,
        out_shape=(
            jax.ShapeDtypeStruct((ROWS, 256), F32),
            jax.ShapeDtypeStruct((ROWS, 256), F32),
            jax.ShapeDtypeStruct((ROWS, 256), F32),
            jax.ShapeDtypeStruct((192, 4096), BF16),
        ),
        in_specs=[hbm] * 9,
        out_specs=[hbm] * 4,
        scratch_shapes=[
            pltpu.VMEM((16, 4096), BF16),
            pltpu.VMEM((1, 4096), F32),
            pltpu.VMEM((192, 256), BF16),
            pltpu.VMEM((1, 128), jnp.int32),
            pltpu.VMEM((1, 128), jnp.int32),
            pltpu.VMEM((2, 4, ROWS, 256), BF16),
            pltpu.VMEM((2, 4, ROWS, 256), BF16),
            pltpu.VMEM((2, ROWS, 256), BF16),
            pltpu.VMEM((2, 2, ROWS, 256), BF16),
            pltpu.VMEM((ROWS, 256), BF16),
            pltpu.VMEM((ROWS, 256), BF16),
            pltpu.VMEM((3, ROWS, 256), F32),
            pltpu.VMEM((ROWS, 256), F32),
            pltpu.VMEM((32, 8, 128), jnp.int32),
            pltpu.VMEM((256, 128), BF16),
            pltpu.VMEM((256, 128), BF16),
            pltpu.VMEM((256, 256), BF16),
            pltpu.VMEM((2, 16, 2048), BF16),
            pltpu.VMEM((2, 8, 16, 256), BF16),
            pltpu.VMEM((2, 8, 32, 256), BF16),
            pltpu.VMEM((8, 2, 32, 256), BF16),
            pltpu.VMEM((2, 32, 256), BF16),
            pltpu.VMEM((32, 256), BF16),
            pltpu.VMEM((2, 32, 256), BF16),
            pltpu.VMEM((2, 8, 32, 256), BF16),
            pltpu.VMEM((3, 1, 128), F32),
            pltpu.VMEM((3, 8, 1, 128), F32),
            pltpu.VMEM((256, 256), BF16),
            pltpu.VMEM((256, 256), BF16),
            pltpu.VMEM((512, 128), BF16),
            pltpu.VMEM((512, 128), BF16),
            pltpu.VMEM((32, 128, 256), BF16),
            pltpu.VMEM((192, 4096), BF16),
            dma((9,)),
            dma((4,)),
            dma((4,)), dma((4,)),
            dma((len(PIECES), 2)), dma((len(PIECES), 2)),
            dma((len(PIECES), 2, 2)), dma((len(PIECES), 2, 2)),
            dma((len(PIECES),)), dma((len(PIECES),)),
            dma((2,)), dma((2,)),
            dma((1,)), dma((1,)),
            dma((6,)), dma((6,)),
            dma((2,)), dma((2,)),
            dma((4,)), dma((4,)),
            dma((2, 4)), dma((2, 4)),
            dma((1,)), dma((1,)),
            dma((2, 4)), dma((2, 4)),
            dma((2, 4, 4)), dma((2, 4, 4)),
            dma((2, 4)), dma((2, 4)),
            dma((2, 4, 4)), dma((2, 4, 4)),
        ],
        compiler_params=pltpu.CompilerParams(
            collective_id=0, has_side_effects=True, vmem_limit_bytes=56 << 20
        ),
        name="step",
    )(
        grad_groups.reshape(2, 4, 2, ROWS, 256),
        master,
        moment1,
        moment2,
        proj,
        ln_gain.reshape(1, 4096),
        w_qkv.T,
        token_owner.reshape(1, 128),
        token_row.reshape(1, 128),
    )
    new_master, new_m1, new_m2, qkv_t = pl.pallas_call(
        store_kernel,
        out_shape=tuple(jax.ShapeDtypeStruct(a.shape, a.dtype) for a in results),
        in_specs=[pl.BlockSpec(memory_space=pl.ANY)] * 4,
        out_specs=[hbm] * 4,
        scratch_shapes=[pltpu.VMEM(a.shape, a.dtype) for a in results] + [dma((2, 5))],
        name="store",
    )(*results)
    return new_master, new_m1, new_m2, qkv_t.T


def solution(mesh):
    placed = (
        P("dp", "shard", None),
        P(("shard", "dp"), None),
        P(("shard", "dp"), None),
        P(("shard", "dp"), None),
        P("dp", None),
        P(),
        P("dp", "shard"),
        P(("dp", "shard"), None),
        P(("dp", "shard")),
    )
    return jax.shard_map(
        body,
        mesh=mesh,
        in_specs=placed,
        out_specs=(
            P(("shard", "dp"), None),
            P(("shard", "dp"), None),
            P(("shard", "dp"), None),
            P("dp", "shard"),
        ),
        check_vma=False,
    )
```
